32 devices in a mesh: groups: 2 (over y), shard: 16 (over z, x, core).
Axes of the slice: x: 2, y: 2, z: 4, core: 2. Of those that a mesh axis runs over, the one named last changes fastest.
Arguments:
- queries: bfloat16 [256, 32, 128], P(('groups', 'shard')), parts along dimension 0, may hold values from -6 to 6
- centroids: bfloat16 [16384, 128], P(('groups', 'shard')), parts along dimension 0, may hold values from -0.5 to 0.5
- passages: bfloat16 [4096, 128, 128], P(('groups', 'shard')), parts along dimension 0, may hold values from -0.5 to 0.5
- lengths: int32 [32, 128], P(('groups', 'shard')), parts along dimension 0, may hold values from 1 to 128, 8192 in all within a row
- cand_owner: int32 [256, 16, 1], P(('groups', 'shard')), parts along dimension 0, may hold values from 0 to 15; in each aligned block of 128 rows (0 to 127, 128 to 255, ..., all dimensions but the last counted through in order) at most 16 rows name the same one
- cand_row: int32 [256, 16], P(('groups', 'shard')), parts along dimension 0, may hold values from 0 to 127
Outputs:
- centroid_best: float32 [256, 32], P(('groups', 'shard')), parts along dimension 0
- maxsim: float32 [256, 16], P(('groups', 'shard')), parts along dimension 0
The draws below stay inside these ranges and needn't reach their ends.
There are 2 independent parts, one for each index of `groups`. The reference program is written for one: setup_inputs(seed, part) draws one part's arguments, and reference() takes and returns one part's arrays. A program takes and returns all parts, laid end to end along the dimension named above; each array names one. Nothing has to cross between parts.
Inputs may be any that keep to these rules, and one draw needn't show every extreme that they name: `cand_owner`: among the 128 candidates of the queries of one device, no owner is named more than 16 times, a bound that some block reaches.
All inputs are finite; a program needn't handle non-finite values.
Results may differ from the reference program's by a relative error of at most 0.0003.
Values may be sent and summed in bfloat16 or wider, within the bound.
No kernel may reach another device: no remote copies, remote signals or barrier semaphores. Data moves between devices by JAX's collectives and lax.ppermute only.
A program may use at most 128 MiB of HBM per device.

```python
import math
import jax
import jax.numpy as jnp
import numpy as np
from jax import lax

DIM = 128
QT = 32
PTOK = 128
CENT_DEV = 512
Q_DEV = 8
CAND = 16
PASS_DEV = 128
QUERIES = 128
CENTROIDS = 8192
PASSAGES = 2048
SLOT = 16
N_SHARD = 16


def set_ends(values, key, low, high):
    spot = [jax.random.randint(jax.random.fold_in(key, axis), (), 0, length) for axis, length in enumerate(values.shape)]
    main_axis = values.shape.index(max(values.shape))
    next_to = spot[:main_axis] + [(spot[main_axis] + 1) % values.shape[main_axis]] + spot[main_axis + 1:]
    return values.at[tuple(spot)].set(low).at[tuple(next_to)].set(high)


def level_of(key, extent, pieces, low, top_value):
    level, own = 1.0, jax.random.fold_in(key, 6)
    for dim, blocks in pieces:
        heights = jnp.exp(jax.random.uniform(jax.random.fold_in(own, dim), (blocks,), jnp.float32, low / len(pieces), top_value / len(pieces)))
        level = level * jnp.repeat(heights, extent[dim] // blocks).reshape([-1 if axis == dim else 1 for axis in range(len(extent))])
    return level


def length_profile(amount, total, most, slope):
    weights = [(1 << 20) // math.isqrt(standing ** slope) + 1 for standing in range(2, amount + 1)]
    rest, counts = total - most - (amount - 1), [1] * (amount - 1)
    while rest > 0:
        movable = [i for i in range(amount - 1) if counts[i] < most]
        mass, left = sum([weights[i] for i in movable]), rest
        for i in movable:
            more = min(most - counts[i], max(1, left * weights[i] // mass), rest)
            counts[i] = counts[i] + more
            rest = rest - more
    return np.array([most] + counts)


def ragged(stream_key, count, total, most, skew):
    if count == 2:
        one = jax.random.randint(stream_key, (), max(1, total - most), min(most, total - 1) + 1)
        return jnp.stack([one, total - one])
    sizes = jnp.asarray(length_profile(count, total, most, skew), jnp.int32)
    twos = (count - 1) // 2
    source_of, taker = sizes[1:1 + 2 * twos:2], sizes[2:2 + 2 * twos:2]
    room = jnp.minimum(source_of - 1, most - taker)
    shifted = jax.random.randint(jax.random.fold_in(stream_key, 1), (twos,), 0, 1 << 20) % (room + 1)
    sizes = sizes.at[1:1 + 2 * twos:2].set(source_of - shifted).at[2:2 + 2 * twos:2].set(taker + shifted)
    return sizes[jax.random.permutation(jax.random.fold_in(stream_key, 2), count)]


def assign_block(rng, own, number, rows, amount, top, bound, skew):
    sequence = jax.random.permutation(rng, amount)
    packed, ordinary = portions_of(amount, rows * top, bound, skew, True), portions_of(amount, rows * top, bound, skew, False)
    places = jnp.arange(amount)

    def named(sizes, offset_by):
        used = int((sizes > 0).sum())
        fixed = max(1, used // 4)
        shifted = fixed + (places - fixed + offset_by * (used - fixed)) % max(1, amount - fixed)
        return jnp.zeros((amount,), jnp.int32).at[sequence[jnp.where(places < fixed, places, shifted)]].set(jnp.asarray(sizes, jnp.int32))

    sizes = jnp.where(number % 4 == 0, named(packed, number // 4), named(ordinary, number - number // 4 - 1))
    mixed = jax.random.permutation(jax.random.fold_in(own, 3), amount)
    donor, receiver = mixed[0:amount // 2 * 2:2], mixed[1:amount // 2 * 2:2]
    margin = jnp.minimum(sizes[donor] - 1, bound - sizes[receiver]) // 2
    margin = jnp.where((donor == sequence[0]) | (receiver == sequence[0]) | (sizes[receiver] == 0), 0, jnp.maximum(margin, 0))
    shifted = jax.random.randint(jax.random.fold_in(own, 4), (amount // 2,), 0, 1 << 20) % (margin + 1)
    sizes = sizes.at[donor].add(-shifted).at[receiver].add(shifted)
    items = jnp.searchsorted(jnp.cumsum(sizes), jnp.arange(rows * top), side="right").astype(jnp.int32)
    listing = items.reshape(top, rows).T
    listing = listing[jax.random.permutation(jax.random.fold_in(own, 1), rows)]
    offset_by = jax.random.randint(jax.random.fold_in(own, 2), (rows, 1), 0, top)
    return jnp.take_along_axis(listing, (jnp.arange(top)[None, :] + offset_by) % top, axis=1)


def portions_of(count, total, bound, slope, full):
    loads = [(1 << 20) // math.isqrt(rank ** slope) + 1 for rank in range(1, count + 1)]
    largest = bound if full else min(bound, max(-(-total // count), total * loads[0] // sum(loads)))
    least = 1 if total - largest >= count - 1 else 0
    given, spare = [largest] + [least] * (count - 1), total - largest - least * (count - 1)
    while spare > 0:
        candidates = [i for i in range(1, count) if given[i] < largest] or [i for i in range(1, count) if given[i] < bound]
        pool, left = sum([loads[i] for i in candidates]), spare
        for i in candidates:
            addition = min(bound - given[i], max(1, left * loads[i] // pool), spare)
            given[i] = given[i] + addition
            spare = spare - addition
    return np.array(given)


def scatter_about(stream_key, dims, deviation, bound, shards=(), kind=jnp.bfloat16):
    values = deviation * jax.random.normal(stream_key, dims, jnp.float32)
    if shards:
        values = values * level_of(stream_key, dims, shards, -0.22, 0.18)
    return jnp.clip(values, -bound, bound).astype(kind)


def setup_inputs(seed: int = 0, part: int = 0) -> dict:
    keys = jax.random.split(jax.random.key(seed), 7)
    part_splits = jax.random.split(jax.random.fold_in(keys[6], part), 7)
    queries = scatter_about(part_splits[0], (QUERIES, QT, DIM), 1.0, 6.0, ((0, 16),))
    centroids = scatter_about(part_splits[1], (CENTROIDS, DIM), DIM ** -0.5, 0.5, ((0, 16),))
    passages = scatter_about(part_splits[2], (PASSAGES, PTOK, DIM), DIM ** -0.5, 0.5, ((0, 16),))
    lengths = jax.vmap(lambda own: ragged(own, PASS_DEV, PTOK // 2 * PASS_DEV, PTOK, 1))(jax.random.split(part_splits[3], N_SHARD)).reshape((N_SHARD, PASS_DEV)).astype(jnp.int32)
    cand_owner_keys = jax.random.split(jax.random.fold_in(part_splits[4], 1), QUERIES * CAND // (Q_DEV * CAND))
    cand_owner_turns = jax.random.permutation(jax.random.fold_in(part_splits[4], 3), QUERIES * CAND // (Q_DEV * CAND))
    cand_owner = jax.vmap(lambda own, number: assign_block(jax.random.fold_in(part_splits[4], 2), own, number, Q_DEV * CAND, N_SHARD, 1, SLOT, 2))(cand_owner_keys, cand_owner_turns).reshape((QUERIES, CAND, 1))
    cand_row = set_ends(jax.random.randint(part_splits[5], (QUERIES, CAND), 0, PASS_DEV), jax.random.fold_in(part_splits[5], 1), 0, PASS_DEV - 1).astype(jnp.int32)
    return dict(queries=queries, centroids=centroids, passages=passages, lengths=lengths, cand_owner=cand_owner, cand_row=cand_row)


def reference(queries, centroids, passages, lengths, cand_owner, cand_row):
    tokens = queries.reshape(QUERIES * QT, DIM)
    cent_blocks = centroids.reshape(N_SHARD, CENT_DEV, DIM)

    def best_step(carry, block):
        scores = jnp.dot(tokens, block.T, preferred_element_type=jnp.float32)
        return jnp.maximum(carry, jnp.max(scores, axis=1)), None

    start_best = jnp.full((QUERIES * QT,), -jnp.inf, dtype=jnp.float32)
    best, _ = lax.scan(best_step, start_best, cent_blocks)
    centroid_best = best.reshape(QUERIES, QT)

    flat_len = lengths.reshape(-1)
    gid = (cand_owner[:, :, 0] * PASS_DEV + cand_row).astype(jnp.int32)

    def one_query(item):
        qtok, ids = item
        blocks = passages[ids]
        blen = flat_len[ids]
        sim = jnp.einsum("td,cpd->ctp", qtok.astype(jnp.float32), blocks.astype(jnp.float32),
                         precision=lax.Precision.HIGHEST)
        valid = jnp.arange(PTOK)[None, :] < blen[:, None]
        sim = jnp.where(valid[:, None, :], sim, jnp.float32(-1e30))
        return jnp.mean(jnp.max(sim, axis=-1), axis=-1)

    maxsim = lax.map(one_query, (queries, gid))
    return centroid_best, maxsim
```

```python
import functools

import jax
import jax.numpy as jnp
from jax import lax
from jax.experimental import pallas as pl
from jax.experimental.pallas import tpu as pltpu
from jax.sharding import PartitionSpec as P

LOW = -1e30
LANES = 128


def pack_kernel(slots, q_ref, owner_ref, row_ref, out_ref):
    q_dev, cand = owner_ref.shape
    tokens = q_ref.shape[0]
    owners = out_ref.shape[0] - tokens
    out_ref[:tokens] = q_ref[...]
    lane = lax.broadcasted_iota(jnp.int32, (q_dev, LANES), 1)
    own_q = lax.broadcasted_iota(jnp.int32, (q_dev, LANES), 0) == lane // cand
    spread = (
        lax.broadcasted_iota(jnp.int32, (cand, LANES), 0)
        == lax.broadcasted_iota(jnp.int32, (cand, LANES), 1) % cand
    ).astype(jnp.float32)

    def flat(ref):
        wide = jnp.dot(ref[...].astype(jnp.float32), spread, preferred_element_type=jnp.float32)
        return jnp.sum(jnp.where(own_q, wide, 0.0), axis=0, keepdims=True)

    owner, row = flat(owner_ref), flat(row_ref)
    number = lax.broadcasted_iota(jnp.int32, (1, LANES), 1).astype(jnp.float32)
    code = row * 256.0 + (number + 1.0)
    hit = lax.broadcasted_iota(jnp.int32, (owners, LANES), 0).astype(jnp.float32) == owner
    earlier = (
        lax.broadcasted_iota(jnp.int32, (LANES, LANES), 0)
        <= lax.broadcasted_iota(jnp.int32, (LANES, LANES), 1)
    ).astype(jnp.float32)
    rank = jnp.dot(hit.astype(jnp.float32), earlier, preferred_element_type=jnp.float32)
    rank = jnp.where(hit, rank, 0.0)
    wide_lane = lax.broadcasted_iota(jnp.int32, (owners, LANES), 1)
    table = jnp.zeros((owners, LANES), jnp.float32)
    for slot in range(slots):
        value = jnp.sum(jnp.where(rank == slot + 1.0, code, 0.0), axis=1, keepdims=True)
        rows = jnp.floor(value * (1.0 / 256.0))
        table = jnp.where(wide_lane == slot, rows, table)
        table = jnp.where(wide_lane == slots + slot, value - rows * 256.0, table)
    out_ref[tokens:] = table.astype(out_ref.dtype)


def score_kernel(slots, cand, qt, all_ref, cent_ref, pass_ref, len_ref, out_ref,
                 held, codes, codes_smem, len_smem, pass_sem, len_sem, code_sem):
    blocks, height, dim = all_ref.shape
    tokens = out_ref.shape[2] - LANES
    owners = height - tokens
    me = lax.axis_index("shard")
    fetch = pltpu.make_async_copy(pass_ref, held, pass_sem)
    fetch.start()
    fetch_len = pltpu.make_async_copy(len_ref, len_smem, len_sem)
    fetch_len.start()
    mine = lax.broadcasted_iota(jnp.int32, (owners, LANES), 0) == me

    def pick(r, _):
        table = all_ref[r, tokens:, :].astype(jnp.float32)
        line = jnp.sum(jnp.where(mine, table, 0.0), axis=0, keepdims=True)
        codes[pl.ds(r, 1), :] = line.astype(jnp.int32)
        return _

    lax.fori_loop(0, blocks, pick, 0, unroll=True)
    send = pltpu.make_async_copy(codes, codes_smem, code_sem)
    send.start()

    def best(r, _):
        rows = all_ref[r, :tokens, :]
        top = None
        step = 128
        for c in range(0, cent_ref.shape[0], step):
            scores = lax.dot_general(
                cent_ref[c:c + step, :], rows, (((1,), (1,)), ((), ())),
                preferred_element_type=jnp.float32)
            part = scores.reshape(step // 8, 8, tokens)
            part = jnp.max(part, axis=0)
            top = part if top is None else jnp.maximum(top, part)
        out_ref[r, :, :tokens] = jnp.max(top, axis=0, keepdims=True)
        return _

    lax.fori_loop(0, blocks, best, 0)
    send.wait()
    fetch_len.wait()
    fetch.wait()
    lane = lax.broadcasted_iota(jnp.int32, (8, LANES), 1)

    def maxsim(r, _):
        total = jnp.full((8, LANES), LOW, jnp.float32)
        for slot in range(slots):
            row = codes_smem[r, slot]
            number = codes_smem[r, slots + slot] - 1
            query = jnp.maximum(number, 0) // cand
            length = len_smem[0, row]
            rows = all_ref[r, pl.ds(pl.multiple_of(query * qt, qt), qt), :]
            sim = lax.dot_general(rows, held[row], (((1,), (1,)), ((), ())),
                                  preferred_element_type=jnp.float32)
            parts = []
            for t in range(0, qt, 8):
                part = jnp.where(lane < length, sim[t:t + 8, :], LOW)
                parts.append(jnp.max(part, axis=1, keepdims=True))
            total = jnp.where(lane == number, sum(parts), total)
        out_ref[r, :, tokens:] = jnp.sum(total, axis=0, keepdims=True) * (1.0 / qt)
        return _

    lax.fori_loop(0, blocks, maxsim, 0)


def last_kernel(a_ref, b_ref, best_ref, sim_ref):
    q_dev, qt = best_ref.shape
    cand = sim_ref.shape[1]
    both = jnp.maximum(a_ref[...], b_ref[...])
    for q in range(q_dev):
        best_ref[q:q + 1, :] = both[:, q * qt:(q + 1) * qt]
        at = q_dev * qt + q * cand
        sim_ref[q:q + 1, :] = both[:, at:at + cand]


def body(queries, centroids, passages, lengths, cand_owner, cand_row):
    q_dev, qt, dim = queries.shape
    cand = cand_row.shape[1]
    shards = lax.axis_size("shard")
    slots = 2 * q_dev * cand // shards
    tokens = q_dev * qt
    vmem = pl.BlockSpec(memory_space=pltpu.VMEM)
    hbm = pl.BlockSpec(memory_space=pl.ANY)
    owners = -(-shards // 16) * 16
    block = pl.pallas_call(
        functools.partial(pack_kernel, slots),
        out_shape=jax.ShapeDtypeStruct((tokens + owners, dim), queries.dtype),
        in_specs=[vmem] * 3,
        out_specs=vmem,
        name="pack",
    )(queries.reshape(tokens, dim), cand_owner.reshape(q_dev, cand), cand_row)

    steps = []
    k = shards // 2
    while k >= 1:
        steps.append(k | 1)
        k //= 2
    held = block[None]
    for k in steps:
        pairs = [(i, i ^ k) for i in range(shards)]
        held = jnp.concatenate([held, lax.ppermute(held, "shard", pairs)], axis=0)

    width = tokens + q_dev * cand
    result = pl.pallas_call(
        functools.partial(score_kernel, slots, cand, qt),
        out_shape=jax.ShapeDtypeStruct((shards, 1, width), jnp.float32),
        in_specs=[vmem, vmem, hbm, hbm],
        out_specs=vmem,
        scratch_shapes=[
            pltpu.VMEM(passages.shape, passages.dtype),
            pltpu.VMEM((shards, LANES), jnp.int32),
            pltpu.SMEM((shards, LANES), jnp.int32),
            pltpu.SMEM(lengths.shape, jnp.int32),
            pltpu.SemaphoreType.DMA,
            pltpu.SemaphoreType.DMA,
            pltpu.SemaphoreType.DMA,
        ],
        compiler_params=pltpu.CompilerParams(vmem_limit_bytes=32 * 1024 * 1024),
        name="score",
    )(held, centroids, passages, lengths)

    for n, k in enumerate(reversed(steps)):
        half = result.shape[0] // 2
        pairs = [(i, i ^ k) for i in range(shards)]
        got = lax.ppermute(result[half:], "shard", pairs)
        if half > 1:
            result = jnp.maximum(result[:half], got)
        else:
            mine = result[:half]
    return pl.pallas_call(
        last_kernel,
        out_shape=(jax.ShapeDtypeStruct((q_dev, qt), jnp.float32), jax.ShapeDtypeStruct((q_dev, cand), jnp.float32)),
        in_specs=[vmem] * 2,
        out_specs=(vmem, vmem),
        name="last",
    )(mine[0], got[0])


def solution(mesh):
    both = ("groups", "shard")
    placed = (P(both, None, None), P(both, None), P(both, None, None), P(both, None), P(both, None, None), P(both, None))
    return jax.shard_map(body, mesh=mesh, in_specs=placed, out_specs=(P(both, None), P(both, None)), check_vma=False)
```

```python
import functools

import jax
import jax.numpy as jnp
from jax import lax
from jax.experimental import pallas as pl
from jax.experimental.pallas import tpu as pltpu
from jax.sharding import PartitionSpec as P

LOW = -1e30
LANES = 128
HEAD = 16
MIB = 1024 * 1024
NT = (((1,), (1,)), ((), ()))


def pack_kernel(slots, q_ref, owner_ref, row_ref, out_ref, owner_held, row_held, sems):
    q_dev, cand = owner_ref.shape
    tokens = q_ref.shape[0]
    owners = out_ref.shape[0] - tokens - HEAD
    copies = [
        pltpu.make_async_copy(source, target, sems.at[n])
        for n, (source, target) in enumerate(
            ((owner_ref, owner_held), (row_ref, row_held), (q_ref, out_ref.at[pl.ds(0, tokens)])))
    ]
    for copy in copies:
        copy.start()
    copies[0].wait()
    copies[1].wait()
    lane = lax.broadcasted_iota(jnp.int32, (q_dev, LANES), 1)
    own_q = lax.broadcasted_iota(jnp.int32, (q_dev, LANES), 0) == lane // cand
    spread = (
        lax.broadcasted_iota(jnp.int32, (cand, LANES), 0)
        == lax.broadcasted_iota(jnp.int32, (cand, LANES), 1) % cand
    ).astype(jnp.float32)

    def flat(ref):
        wide = jnp.dot(ref[...].astype(jnp.float32), spread, preferred_element_type=jnp.float32)
        return jnp.sum(jnp.where(own_q, wide, 0.0), axis=0, keepdims=True)

    owner, row = flat(owner_held), flat(row_held)
    query = (lax.broadcasted_iota(jnp.int32, (1, LANES), 1) // cand).astype(jnp.float32)
    code = row * 256.0 + query
    hit = lax.broadcasted_iota(jnp.int32, (owners, LANES), 0).astype(jnp.float32) == owner
    earlier = (
        lax.broadcasted_iota(jnp.int32, (LANES, LANES), 0)
        < lax.broadcasted_iota(jnp.int32, (LANES, LANES), 1)
    ).astype(jnp.float32)
    rank = jnp.dot(hit.astype(jnp.float32), earlier, preferred_element_type=jnp.float32)
    rank = jnp.where(hit, rank, -1.0)
    wide_lane = lax.broadcasted_iota(jnp.int32, (owners, LANES), 1)
    table = jnp.zeros((owners, LANES), jnp.float32)
    for slot in range(slots):
        value = jnp.sum(jnp.where(rank == float(slot), code, 0.0), axis=1, keepdims=True)
        rows = jnp.floor(value * (1.0 / 256.0))
        table = jnp.where(wide_lane == slot, rows, table)
        table = jnp.where(wide_lane == slots + slot, value - rows * 256.0, table)
    own_rank = jnp.max(rank, axis=0, keepdims=True)
    head = lax.broadcasted_iota(jnp.int32, (HEAD, LANES), 0)
    out_ref[tokens:tokens + HEAD] = jnp.where(head == 0, owner, jnp.where(head == 1, own_rank, 0.0)).astype(out_ref.dtype)
    out_ref[tokens + HEAD:] = table.astype(out_ref.dtype)
    copies[2].wait()


def fetch_kernel(cent_ref, pass_ref, len_ref, cent_out, pass_out, len_out, sems):
    copies = [
        pltpu.make_async_copy(source, target, sems.at[n])
        for n, (source, target) in enumerate(((cent_ref, cent_out), (pass_ref, pass_out), (len_ref, len_out)))
    ]
    for copy in copies:
        copy.start()
    for copy in copies:
        copy.wait()


def score_kernel(slots, qt, counts, *refs):
    parts = len(counts)
    all_refs, (cent_ref, held, len_ref), out_refs = refs[:parts], refs[parts:parts + 3], refs[parts + 3:]
    height = all_refs[0].shape[1]
    tokens = out_refs[0].shape[2] - LANES
    owners = height - tokens - HEAD
    at = tokens + HEAD
    ptok = held.shape[1]
    me = lax.axis_index("shard")
    mine = lax.broadcasted_iota(jnp.int32, (owners, LANES), 0) == me
    lens = jnp.broadcast_to(len_ref[...], (8, LANES))
    place = lax.broadcasted_iota(jnp.int32, (ptok, qt), 0)

    def group(ref, out, start, count):
        lines = []
        for n in range(count):
            table = ref[start + n, at:, :].astype(jnp.float32)
            lines.append(jnp.sum(jnp.where(mine, table, 0.0), axis=0, keepdims=True))
        lines.extend([jnp.zeros((1, LANES), jnp.float32)] * (8 - count))
        row = jnp.concatenate(lines, axis=0).astype(jnp.int32)
        query = pltpu.roll(row, LANES - slots, 1)
        length = jnp.take_along_axis(lens, row, axis=1)
        codes = row + (query << 8) + (length << 16)
        for n in range(count):
            r = start + n
            scores = lax.dot_general(cent_ref[...], ref[r, :tokens, :], NT, preferred_element_type=jnp.float32)
            top = jnp.max(scores.reshape(-1, 8, tokens), axis=0)
            out[r, :, :tokens] = jnp.max(top, axis=0, keepdims=True)
        for n in range(count):
            r = start + n
            head = ref[r, tokens:at, :].astype(jnp.float32)
            rank = jnp.where(head[0:1, :] == me.astype(jnp.float32), head[1:2, :], -1.0)
            total = jnp.full((1, LANES), LOW, jnp.float32)
            for slot in range(slots):
                code = codes[n, slot]
                first = pl.multiple_of(((code >> 8) & 255) * qt, qt)
                sim = lax.dot_general(held[code & 255], ref[r, pl.ds(first, qt), :], NT,
                                      preferred_element_type=jnp.float32)
                sim = jnp.where(place < (code >> 16), sim, LOW)
                top = jnp.max(jnp.max(sim.reshape(-1, 8, qt), axis=0), axis=0, keepdims=True)
                score = jnp.sum(top, axis=1, keepdims=True) * (1.0 / qt)
                total = jnp.where(rank == float(slot), score, total)
            out[r, :, tokens:] = total

    for count, ref, out in zip(counts, all_refs, out_refs):
        size = min(count, 8)
        if count == size:
            group(ref, out, 0, count)
        else:

            def some(g, _, ref=ref, out=out, size=size):
                group(ref, out, g * size, size)
                return _

            lax.fori_loop(0, count // size, some, 0)


def last_kernel(a_ref, b_ref, best_ref, sim_ref):
    q_dev, qt = best_ref.shape
    cand = sim_ref.shape[1]
    both = jnp.maximum(a_ref[0], b_ref[0])
    for q in range(q_dev):
        best_ref[q:q + 1, :] = both[:, q * qt:(q + 1) * qt]
        at = q_dev * qt + q * cand
        sim_ref[q:q + 1, :] = both[:, at:at + cand]


def body(queries, centroids, passages, lengths, cand_owner, cand_row):
    q_dev, qt, dim = queries.shape
    cand = cand_row.shape[1]
    shards = lax.axis_size("shard")
    slots = 2 * q_dev * cand // shards
    tokens = q_dev * qt
    vmem = pl.BlockSpec(memory_space=pltpu.VMEM)
    hbm = pl.BlockSpec(memory_space=pltpu.HBM)
    owners = -(-shards // 16) * 16
    height = tokens + HEAD + owners

    def stay(x):
        return pltpu.with_memory_space_constraint(x, pltpu.HBM)

    block = pl.pallas_call(
        functools.partial(pack_kernel, slots),
        out_shape=pltpu.VMEM((height, dim), queries.dtype),
        in_specs=[hbm] * 3,
        out_specs=vmem,
        scratch_shapes=[
            pltpu.VMEM((q_dev, cand), jnp.int32),
            pltpu.VMEM((q_dev, cand), jnp.int32),
            pltpu.SemaphoreType.DMA((3,)),
        ],
        compiler_params=pltpu.CompilerParams(vmem_limit_bytes=2 * MIB),
        name="pack",
    )(stay(queries.reshape(tokens, dim)), stay(cand_owner.reshape(q_dev, cand)), stay(cand_row))

    index = pl.pallas_call(
        fetch_kernel,
        out_shape=[pltpu.VMEM(x.shape, x.dtype) for x in (centroids, passages, lengths)],
        in_specs=[hbm] * 3,
        out_specs=[vmem] * 3,
        scratch_shapes=[pltpu.SemaphoreType.DMA((3,))],
        compiler_params=pltpu.CompilerParams(vmem_limit_bytes=MIB),
        name="fetch",
    )(stay(centroids), stay(passages), stay(lengths))

    def swap(x, k):
        return lax.ppermute(x, "shard", [(i, i ^ k) for i in range(shards)])

    def score(*blocks):
        counts = tuple(b.shape[0] for b in blocks)
        total = sum(counts)
        return pl.pallas_call(
            functools.partial(score_kernel, slots, qt, counts),
            out_shape=[pltpu.VMEM((n, 1, tokens + q_dev * cand), jnp.float32) for n in counts],
            in_specs=[vmem] * (len(blocks) + 3),
            out_specs=[vmem] * len(blocks),
            compiler_params=pltpu.CompilerParams(vmem_limit_bytes=4 * MIB),
            cost_estimate=pl.CostEstimate(
                flops=4 * total * (tokens * centroids.size + slots * qt * (passages.size // passages.shape[0])),
                bytes_accessed=total * MIB, transcendentals=0),
            name="score",
        )(*blocks, *index)

    far = []
    k = shards // 2
    while k > 2:
        far.append(k | 1)
        k //= 2
    first = block[None]
    for k in far[:-2]:
        first = jnp.concatenate([first, swap(first, k)], axis=0)
    second = swap(first, far[-2])
    third = swap(first, far[-1])
    xa = swap(first, 3)
    second, index = lax.optimization_barrier((second, index))
    fourth = swap(second, far[-1])
    near3 = jnp.concatenate([second, third], axis=0)
    xb = swap(near3, 3)
    c1 = swap(jnp.concatenate([first, near3], axis=0), 1)
    s1 = score(first, near3)
    fourth, s1 = lax.optimization_barrier((fourth, s1))
    xc = swap(fourth, 3)
    c2 = swap(jnp.concatenate([fourth, xa], axis=0), 1)
    s2 = score(fourth, xa, c1)
    xb, s2 = lax.optimization_barrier((xb, s2))
    c3 = swap(xb, 1)
    s3 = score(c2, xb)
    xc, s3 = lax.optimization_barrier((xc, s3))
    c4 = swap(xc, 1)
    s4 = score(c3)
    c4, s4 = lax.optimization_barrier((c4, s4))
    s5 = score(c4)
    other = jnp.concatenate([s2[2], s3[0], s4[0], s5[0]], axis=0)
    got = swap(other, 1)
    s6 = score(xc)
    near = jnp.concatenate([s1[0], s1[1], s2[0], s2[1], s3[1], s6[0]], axis=0)
    result = jnp.maximum(near, got)
    for k in [3] + far[::-1]:
        half = result.shape[0] // 2
        got = swap(result[half:], k)
        if half > 1:
            result = jnp.maximum(result[:half], got)
        else:
            mine = result[:half]
    return pl.pallas_call(
        last_kernel,
        out_shape=(jax.ShapeDtypeStruct((q_dev, qt), jnp.float32), jax.ShapeDtypeStruct((q_dev, cand), jnp.float32)),
        in_specs=[vmem] * 2,
        out_specs=(vmem, vmem),
        compiler_params=pltpu.CompilerParams(vmem_limit_bytes=MIB),
        name="last",
    )(mine, got)


def solution(mesh):
    both = ("groups", "shard")
    placed = (P(both, None, None), P(both, None), P(both, None, None), P(both, None), P(both, None, None), P(both, None))
    return jax.shard_map(body, mesh=mesh, in_specs=placed, out_specs=(P(both, None), P(both, None)), check_vma=False)
```

```python
import functools

import jax
import jax.numpy as jnp
from jax import lax
from jax.experimental import pallas as pl
from jax.experimental.pallas import tpu as pltpu
from jax.sharding import PartitionSpec as P

LOW = -1e30
LANES = 128
HEAD = 16
MIB = 1024 * 1024
NT = (((1,), (1,)), ((), ()))


def pack_kernel(slots, q_ref, owner_ref, row_ref, out_ref, owner_held, row_held, sems):
    q_dev, cand = owner_ref.shape
    tokens = q_ref.shape[0]
    owners = out_ref.shape[0] - tokens - HEAD
    copies = [
        pltpu.make_async_copy(source, target, sems.at[n])
        for n, (source, target) in enumerate(
            ((owner_ref, owner_held), (row_ref, row_held), (q_ref, out_ref.at[pl.ds(0, tokens)])))
    ]
    for copy in copies:
        copy.start()
    copies[0].wait()
    copies[1].wait()
    lane = lax.broadcasted_iota(jnp.int32, (q_dev, LANES), 1)
    own_q = lax.broadcasted_iota(jnp.int32, (q_dev, LANES), 0) == lane // cand
    spread = (
        lax.broadcasted_iota(jnp.int32, (cand, LANES), 0)
        == lax.broadcasted_iota(jnp.int32, (cand, LANES), 1) % cand
    ).astype(jnp.float32)

    def flat(ref):
        wide = jnp.dot(ref[...].astype(jnp.float32), spread, preferred_element_type=jnp.float32)
        return jnp.sum(jnp.where(own_q, wide, 0.0), axis=0, keepdims=True)

    owner, row = flat(owner_held), flat(row_held)
    query = (lax.broadcasted_iota(jnp.int32, (1, LANES), 1) // cand).astype(jnp.float32)
    code = row * 256.0 + query
    hit = lax.broadcasted_iota(jnp.int32, (owners, LANES), 0).astype(jnp.float32) == owner
    earlier = (
        lax.broadcasted_iota(jnp.int32, (LANES, LANES), 0)
        < lax.broadcasted_iota(jnp.int32, (LANES, LANES), 1)
    ).astype(jnp.float32)
    rank = jnp.dot(hit.astype(jnp.float32), earlier, preferred_element_type=jnp.float32)
    rank = jnp.where(hit, rank, -1.0)
    wide_lane = lax.broadcasted_iota(jnp.int32, (owners, LANES), 1)
    table = jnp.zeros((owners, LANES), jnp.float32)
    for slot in range(slots):
        value = jnp.sum(jnp.where(rank == float(slot), code, 0.0), axis=1, keepdims=True)
        rows = jnp.floor(value * (1.0 / 256.0))
        table = jnp.where(wide_lane == slot, rows, table)
        table = jnp.where(wide_lane == slots + slot, value - rows * 256.0, table)
    own_rank = jnp.max(rank, axis=0, keepdims=True)
    head = lax.broadcasted_iota(jnp.int32, (HEAD, LANES), 0)
    out_ref[tokens:tokens + HEAD] = jnp.where(head == 0, owner, jnp.where(head == 1, own_rank, 0.0)).astype(out_ref.dtype)
    out_ref[tokens + HEAD:] = table.astype(out_ref.dtype)
    copies[2].wait()


def score_kernel(slots, qt, counts, *refs):
    parts = len(counts)
    all_refs, (cent_ref, held, len_ref), out_refs = refs[:parts], refs[parts:parts + 3], refs[parts + 3:]
    height = all_refs[0].shape[1]
    tokens = out_refs[0].shape[2] - LANES
    owners = height - tokens - HEAD
    at = tokens + HEAD
    ptok = held.shape[1]
    me = lax.axis_index("shard")
    mine = lax.broadcasted_iota(jnp.int32, (owners, LANES), 0) == me
    lens = jnp.broadcast_to(len_ref[...], (8, LANES))
    place = lax.broadcasted_iota(jnp.int32, (ptok, qt), 0)

    def group(ref, out, start, count):
        lines = []
        for n in range(count):
            table = ref[start + n, at:, :].astype(jnp.float32)
            lines.append(jnp.sum(jnp.where(mine, table, 0.0), axis=0, keepdims=True))
        lines.extend([jnp.zeros((1, LANES), jnp.float32)] * (8 - count))
        row = jnp.concatenate(lines, axis=0).astype(jnp.int32)
        query = pltpu.roll(row, LANES - slots, 1)
        length = jnp.take_along_axis(lens, row, axis=1)
        codes = row + (query << 8) + (length << 16)
        for n in range(count):
            r = start + n
            scores = lax.dot_general(cent_ref[...], ref[r, :tokens, :], NT, preferred_element_type=jnp.float32)
            top = jnp.max(scores.reshape(-1, 8, tokens), axis=0)
            out[r, :, :tokens] = jnp.max(top, axis=0, keepdims=True)
        for n in range(count):
            r = start + n
            head = ref[r, tokens:at, :].astype(jnp.float32)
            rank = jnp.where(head[0:1, :] == me.astype(jnp.float32), head[1:2, :], -1.0)
            total = jnp.full((1, LANES), LOW, jnp.float32)
            for slot in range(slots):
                code = codes[n, slot]
                first = pl.multiple_of(((code >> 8) & 255) * qt, qt)
                sim = lax.dot_general(held[code & 255], ref[r, pl.ds(first, qt), :], NT,
                                      preferred_element_type=jnp.float32)
                sim = jnp.where(place < (code >> 16), sim, LOW)
                top = jnp.max(jnp.max(sim.reshape(-1, 8, qt), axis=0), axis=0, keepdims=True)
                score = jnp.sum(top, axis=1, keepdims=True) * (1.0 / qt)
                total = jnp.where(rank == float(slot), score, total)
            out[r, :, tokens:] = total

    for count, ref, out in zip(counts, all_refs, out_refs):
        size = min(count, 8)
        if count == size:
            group(ref, out, 0, count)
        else:

            def some(g, _, ref=ref, out=out, size=size):
                group(ref, out, g * size, size)
                return _

            lax.fori_loop(0, count // size, some, 0)


def last_kernel(a_ref, b_ref, best_ref, sim_ref):
    q_dev, qt = best_ref.shape
    cand = sim_ref.shape[1]
    both = jnp.maximum(a_ref[0], b_ref[0])
    for q in range(q_dev):
        best_ref[q:q + 1, :] = both[:, q * qt:(q + 1) * qt]
        at = q_dev * qt + q * cand
        sim_ref[q:q + 1, :] = both[:, at:at + cand]


def body(queries, centroids, passages, lengths, cand_owner, cand_row):
    q_dev, qt, dim = queries.shape
    cand = cand_row.shape[1]
    shards = lax.axis_size("shard")
    slots = 2 * q_dev * cand // shards
    tokens = q_dev * qt
    vmem = pl.BlockSpec(memory_space=pltpu.VMEM)
    hbm = pl.BlockSpec(memory_space=pltpu.HBM)
    owners = -(-shards // 16) * 16
    height = tokens + HEAD + owners

    def stay(x):
        return pltpu.with_memory_space_constraint(x, pltpu.HBM)

    block = pl.pallas_call(
        functools.partial(pack_kernel, slots),
        out_shape=pltpu.VMEM((height, dim), queries.dtype),
        in_specs=[hbm] * 3,
        out_specs=vmem,
        scratch_shapes=[
            pltpu.VMEM((q_dev, cand), jnp.int32),
            pltpu.VMEM((q_dev, cand), jnp.int32),
            pltpu.SemaphoreType.DMA((3,)),
        ],
        compiler_params=pltpu.CompilerParams(vmem_limit_bytes=2 * MIB),
        cost_estimate=pl.CostEstimate(flops=int(1e10), bytes_accessed=1000, transcendentals=0),
        name="pack",
    )(stay(queries.reshape(tokens, dim)), stay(cand_owner.reshape(q_dev, cand)), stay(cand_row))

    index = tuple(pltpu.with_memory_space_constraint(x, pltpu.VMEM) for x in (centroids, passages, lengths))

    def swap(x, k):
        return lax.ppermute(x, "shard", [(i, i ^ k) for i in range(shards)])

    def score(*blocks):
        counts = tuple(b.shape[0] for b in blocks)
        total = sum(counts)
        return pl.pallas_call(
            functools.partial(score_kernel, slots, qt, counts),
            out_shape=[pltpu.VMEM((n, 1, tokens + q_dev * cand), jnp.float32) for n in counts],
            in_specs=[vmem] * (len(blocks) + 3),
            out_specs=[vmem] * len(blocks),
            compiler_params=pltpu.CompilerParams(vmem_limit_bytes=4 * MIB),
            cost_estimate=pl.CostEstimate(
                flops=4 * total * (tokens * centroids.size + slots * qt * (passages.size // passages.shape[0])),
                bytes_accessed=total * MIB, transcendentals=0),
            name="score",
        )(*blocks, *index)

    far = []
    k = shards // 2
    while k > 2:
        far.append(k | 1)
        k //= 2
    first = block[None]
    for k in far[:-2]:
        first = jnp.concatenate([first, swap(first, k)], axis=0)
    f, g = far[-2:]
    d = g ^ 3 ^ 1
    piece = {0: first}
    for k in (f, 3, g, d):
        piece[k] = swap(first, k)
    for k in (d, 3, g):
        piece[f ^ k] = swap(piece[f], k)
    m = first.shape[0]
    score_of = {}

    def cut(x, keys):
        return {k: x[n * m:(n + 1) * m] for n, k in enumerate(keys)}

    def join(table, keys):
        return jnp.concatenate([table[k] for k in keys], axis=0)

    def across(keys):
        return swap(join(piece, keys), 1)

    xa, xb = (3, d), (f ^ d, f ^ 3)
    early = (0, f, g, 3, d)
    scores = score(*(piece[k] for k in early))
    scores, piece[xb[0]], piece[xb[1]] = lax.optimization_barrier((scores, piece[xb[0]], piece[xb[1]]))
    score_of.update(zip(early, scores))
    ca, cb = across(xa), across(xb)
    *scores, ca = score(*(piece[k] for k in xb), ca)
    score_of.update(zip(xb, scores))
    score_of.update(cut(ca, [k ^ 1 for k in xa]))
    ca, cb = lax.optimization_barrier((ca, cb))
    score_of.update(cut(score(cb)[0], [k ^ 1 for k in xb]))

    def back(keys, k):
        got = cut(swap(join(score_of, [key ^ k for key in keys]), k), keys)
        return lambda: {key: jnp.maximum(score_of[key], got[key]) for key in keys}

    column = (0, f, g, f ^ g)
    near = column + tuple(k ^ 1 for k in column)
    take = back(near, 3)
    rest = (f ^ g, *(k ^ 1 for k in column))
    cc = across(column)
    sd = score(piece[f ^ g], cc)
    score_of[f ^ g] = sd[0]
    score_of.update(cut(sd[1], rest[1:]))
    score_of = take()
    score_of = back((0, f, 1, f ^ 1), g)()
    score_of = back((0, 1), f)()
    mine, other = score_of[0], score_of[1]
    for k in far[:-2][::-1]:
        half = mine.shape[0] // 2
        got = swap(jnp.concatenate([mine[half:], other[half:]], axis=0), k)
        mine, other = jnp.maximum(mine[:half], got[:half]), jnp.maximum(other[:half], got[half:])
    got = swap(other, 1)
    return pl.pallas_call(
        last_kernel,
        out_shape=(jax.ShapeDtypeStruct((q_dev, qt), jnp.float32), jax.ShapeDtypeStruct((q_dev, cand), jnp.float32)),
        in_specs=[vmem] * 2,
        out_specs=(vmem, vmem),
        compiler_params=pltpu.CompilerParams(vmem_limit_bytes=MIB),
        name="last",
    )(mine, got)


def solution(mesh):
    both = ("groups", "shard")
    placed = (P(both, None, None), P(both, None), P(both, None, None), P(both, None), P(both, None, None), P(both, None))
    return jax.shard_map(body, mesh=mesh, in_specs=placed, out_specs=(P(both, None), P(both, None)), check_vma=False)
```

```python
import functools
import math

import jax
import jax.numpy as jnp
from jax import lax
from jax.experimental import pallas as pl
from jax.experimental.pallas import tpu as pltpu
from jax.sharding import PartitionSpec as P

LOW = -1e30
LANES = 128
MIB = 1024 * 1024
NT = (((1,), (1,)), ((), ()))


def pack_kernel(slots, q_ref, owner_ref, row_ref, out_ref, owner_held, row_held, sems):
    q_dev, cand = owner_ref.shape
    tokens = q_ref.shape[0]
    owners = out_ref.shape[0] - tokens
    copies = [
        pltpu.make_async_copy(source, target, sems.at[n])
        for n, (source, target) in enumerate(
            ((owner_ref, owner_held), (row_ref, row_held), (q_ref, out_ref.at[pl.ds(0, tokens)])))
    ]
    for copy in copies:
        copy.start()
    lane = lax.broadcasted_iota(jnp.int32, (q_dev, LANES), 1)
    own_q = lax.broadcasted_iota(jnp.int32, (q_dev, LANES), 0) == lane // cand
    spread = (
        lax.broadcasted_iota(jnp.int32, (cand, LANES), 0)
        == lax.broadcasted_iota(jnp.int32, (cand, LANES), 1) % cand
    ).astype(jnp.float32)
    earlier = (
        lax.broadcasted_iota(jnp.int32, (LANES, LANES), 0)
        < lax.broadcasted_iota(jnp.int32, (LANES, LANES), 1)
    ).astype(jnp.float32)
    number = lax.broadcasted_iota(jnp.int32, (1, LANES), 1).astype(jnp.float32) + 1.0
    each = lax.broadcasted_iota(jnp.int32, (owners, LANES), 0).astype(jnp.float32)
    place = lax.broadcasted_iota(jnp.int32, (LANES, LANES), 0).astype(jnp.float32)
    copies[0].wait()
    copies[1].wait()
    both = jnp.concatenate([owner_held[...], row_held[...]], axis=0).astype(jnp.float32)
    wide = jnp.dot(both, spread, preferred_element_type=jnp.float32)
    owner = jnp.sum(jnp.where(own_q, wide[:q_dev], 0.0), axis=0, keepdims=True)
    row = jnp.sum(jnp.where(own_q, wide[q_dev:], 0.0), axis=0, keepdims=True)
    hit = each == owner
    rank = jnp.dot(hit.astype(jnp.float32), earlier, preferred_element_type=jnp.float32)
    rank = jnp.sum(jnp.where(hit, rank, 0.0), axis=0, keepdims=True)
    rows = lax.dot_general(jnp.where(hit, row, 0.0), (place == rank).astype(jnp.float32), NT,
                           preferred_element_type=jnp.float32)
    numbers = lax.dot_general(jnp.where(hit, number, 0.0), (place == rank + slots).astype(jnp.float32), NT,
                              preferred_element_type=jnp.float32)
    out_ref[tokens:] = (rows + numbers).astype(out_ref.dtype)
    copies[2].wait()


def score_kernel(slots, qt, cand, jobs, outs, *refs):
    parts = len(jobs)
    all_refs, (cent_ref, held, len_ref) = refs[:parts], refs[parts:parts + 3]
    out_refs = refs[parts + 3:]
    out_refs = out_refs[len(out_refs) - outs:]
    height = all_refs[0].shape[1]
    tokens = out_refs[0].shape[2] - LANES
    owners = height - tokens
    ptok = held.shape[1]
    me = lax.axis_index("shard")
    mine = lax.broadcasted_iota(jnp.int32, (owners, LANES), 0) == me
    lens = jnp.broadcast_to(len_ref[...], (8, LANES))
    place = lax.broadcasted_iota(jnp.int32, (ptok, qt), 0)
    lane = lax.broadcasted_iota(jnp.int32, (1, LANES), 1) + 1

    def group(blocks):
        lines = []
        for ref, r, _, _ in blocks:
            table = ref[r, tokens:, :].astype(jnp.float32)
            lines.append(jnp.sum(jnp.where(mine, table, 0.0), axis=0, keepdims=True))
        lines.extend([jnp.zeros((1, LANES), jnp.float32)] * (8 - len(blocks)))
        lines = jnp.concatenate(lines, axis=0)
        row = lines.astype(jnp.int32)
        length = jnp.take_along_axis(lens, row, axis=1)
        number = pltpu.roll(lines, LANES - slots, 1)
        query = jnp.maximum(jnp.floor((number - 0.5) * (1.0 / cand)), 0.0).astype(jnp.int32)
        codes = row + (query << 8) + (number.astype(jnp.int32) << 16) + ((length - 1) << 24)
        for ref, r, out, at in blocks:
            scores = lax.dot_general(cent_ref[...], ref[r, :tokens, :], NT, preferred_element_type=jnp.float32)
            top = jnp.max(scores.reshape(-1, 8, tokens), axis=0)
            out[at, :, :tokens] = jnp.max(top, axis=0, keepdims=True)
        for n, (ref, r, out, at) in enumerate(blocks):
            total = jnp.full((1, LANES), LOW, jnp.float32)
            for slot in range(slots):
                code = codes[n, slot]
                first = pl.multiple_of(((code >> 8) & 255) * qt, qt)
                sim = lax.dot_general(held[code & 255], ref[r, pl.ds(first, qt), :], NT,
                                      preferred_element_type=jnp.float32)
                sim = jnp.where(place <= (code >> 24), sim, LOW)
                top = jnp.max(jnp.max(sim.reshape(-1, 8, qt), axis=0), axis=0, keepdims=True)
                score = jnp.sum(top, axis=1, keepdims=True) * (1.0 / qt)
                total = jnp.where(lane == ((code >> 16) & 255), score, total)
            out[at, :, tokens:] = total

    pieces = []
    for ref, job in zip(all_refs, jobs):
        count = ref.shape[0] // len(job)
        pieces.extend((ref, n * count, out_refs[which], at, count) for n, (which, at) in enumerate(job))
    blocks = [(ref, r + n, out, at + n) for ref, r, out, at, count in pieces for n in range(count)]
    if len(blocks) <= 8:
        group(blocks)
        return
    for ref, r, out, at, count in pieces:
        size = math.gcd(count, 8)

        def some(g, _, ref=ref, r=r, out=out, at=at, size=size):
            group([(ref, r + g * size + n, out, at + g * size + n) for n in range(size)])
            return _

        lax.fori_loop(0, count // size, some, 0)


def last_kernel(a_ref, b_ref, best_ref, sim_ref, best, sim, sems):
    q_dev, qt = best.shape
    cand = sim.shape[1]
    both = jnp.maximum(a_ref[0], b_ref[0])
    for q in range(q_dev):
        best[q:q + 1, :] = both[:, q * qt:(q + 1) * qt]
    copies = [pltpu.make_async_copy(best, best_ref, sems.at[0]), pltpu.make_async_copy(sim, sim_ref, sems.at[1])]
    copies[0].start()
    for q in range(q_dev):
        at = q_dev * qt + q * cand
        sim[q:q + 1, :] = both[:, at:at + cand]
    copies[1].start()
    for copy in copies:
        copy.wait()


def body(queries, centroids, passages, lengths, cand_owner, cand_row):
    q_dev, qt, dim = queries.shape
    cand = cand_row.shape[1]
    shards = lax.axis_size("shard")
    slots = 2 * q_dev * cand // shards
    tokens = q_dev * qt
    vmem = pl.BlockSpec(memory_space=pltpu.VMEM)
    hbm = pl.BlockSpec(memory_space=pltpu.HBM)
    owners = -(-shards // 16) * 16
    height = tokens + owners

    def stay(x):
        return pltpu.with_memory_space_constraint(x, pltpu.HBM)

    block = pl.pallas_call(
        functools.partial(pack_kernel, slots),
        out_shape=pltpu.VMEM((height, dim), queries.dtype),
        in_specs=[hbm] * 3,
        out_specs=vmem,
        scratch_shapes=[
            pltpu.VMEM((q_dev, cand), jnp.int32),
            pltpu.VMEM((q_dev, cand), jnp.int32),
            pltpu.SemaphoreType.DMA((3,)),
        ],
        compiler_params=pltpu.CompilerParams(vmem_limit_bytes=2 * MIB),
        cost_estimate=pl.CostEstimate(flops=int(1e10), bytes_accessed=1000, transcendentals=0),
        name="pack",
    )(stay(queries.reshape(tokens, dim)), stay(cand_owner.reshape(q_dev, cand)), stay(cand_row))

    index = tuple(pltpu.with_memory_space_constraint(x, pltpu.VMEM) for x in (centroids, passages, lengths))

    def swap(x, k):
        return lax.ppermute(x, "shard", [(i, i ^ k) for i in range(shards)])

    def score(blocks, jobs, *held):
        total = sum(b.shape[0] for b in blocks)
        wide = pltpu.VMEM((shards // 2, 1, tokens + q_dev * cand), jnp.float32)
        outs = len(held) or 2
        return pl.pallas_call(
            functools.partial(score_kernel, slots, qt, cand, jobs, outs),
            out_shape=[wide] * outs,
            in_specs=[vmem] * (len(blocks) + 3 + len(held)),
            out_specs=[vmem] * outs,
            input_output_aliases={len(blocks) + 3 + n: n for n in range(len(held))},
            compiler_params=pltpu.CompilerParams(vmem_limit_bytes=4 * MIB),
            cost_estimate=pl.CostEstimate(
                flops=4 * total * (tokens * centroids.size + slots * qt * (passages.size // passages.shape[0])),
                bytes_accessed=total * MIB, transcendentals=0),
            name="score",
        )(*blocks, *index, *held)

    far = []
    k = shards // 2
    while k > 2:
        far.append(k | 1)
        k //= 2
    first = block[None]
    for k in far[:-2]:
        first = jnp.concatenate([first, swap(first, k)], axis=0)
    f, g = far[-2:]
    d = g ^ 3 ^ 1
    piece = {0: first}
    for k in (f, 3, g, d):
        piece[k] = swap(first, k)
    for k in (d, 3, g):
        piece[f ^ k] = swap(piece[f], k)
    m = first.shape[0]

    def across(keys):
        return swap(jnp.concatenate([piece[k] for k in keys], axis=0), 1)

    column = (0, 1, f, f ^ 1, g, g ^ 1, f ^ g, f ^ g ^ 1)
    place = {k: (0, n * m) for n, k in enumerate(column)}
    place.update({k ^ 3: (1, n * m) for n, k in enumerate(column)})

    def jobs(*keys):
        return tuple(tuple(place[k] for k in (key if isinstance(key, tuple) else (key,))) for key in keys)

    def only(first, *keys):
        return tuple(tuple((0, at) for _, at in job) for job in jobs(first, *keys))

    xa, xb = (3, d), (f ^ d, f ^ 3)
    early = (0, f, g, 3, d)
    near, beyond = score([piece[k] for k in early], jobs(*early))
    beyond, piece[xb[0]], piece[xb[1]] = lax.optimization_barrier((beyond, piece[xb[0]], piece[xb[1]]))
    ca, cb = across(xa), across(xb)
    [beyond] = score([ca[:m], *(piece[k] for k in xb)], only(xa[0] ^ 1, *xb), beyond)
    beyond, cb = lax.optimization_barrier((beyond, cb))
    [beyond] = score([ca[m:], cb], only(xa[1] ^ 1, tuple(k ^ 1 for k in xb)), beyond)

    got = swap(beyond, 3)
    own = (0, f, g, f ^ g)
    cc = across(own)
    [near] = score([piece[f ^ g], cc], only(f ^ g, tuple(k ^ 1 for k in own)), near)
    near = jnp.maximum(near, got)
    for k in (g, f):
        half = near.shape[0] // 2
        near = jnp.maximum(near[:half], swap(near[half:], k))
    near = near.reshape(2, m, *near.shape[1:])
    for k in far[:-2][::-1]:
        half = near.shape[1] // 2
        near = jnp.maximum(near[:, :half], swap(near[:, half:], k))
    mine, got = near[0], swap(near[1], 1)
    return pl.pallas_call(
        last_kernel,
        out_shape=(jax.ShapeDtypeStruct((q_dev, qt), jnp.float32), jax.ShapeDtypeStruct((q_dev, cand), jnp.float32)),
        in_specs=[vmem] * 2,
        out_specs=(hbm, hbm),
        scratch_shapes=[
            pltpu.VMEM((q_dev, qt), jnp.float32),
            pltpu.VMEM((q_dev, cand), jnp.float32),
            pltpu.SemaphoreType.DMA((2,)),
        ],
        compiler_params=pltpu.CompilerParams(vmem_limit_bytes=MIB),
        name="last",
    )(mine, got)


def solution(mesh):
    both = ("groups", "shard")
    placed = (P(both, None, None), P(both, None), P(both, None, None), P(both, None), P(both, None, None), P(both, None))
    return jax.shard_map(body, mesh=mesh, in_specs=placed, out_specs=(P(both, None), P(both, None)), check_vma=False)
```

```python
import functools
import math

import jax
import jax.numpy as jnp
from jax import lax
from jax.experimental import pallas as pl
from jax.experimental.pallas import tpu as pltpu
from jax.sharding import PartitionSpec as P

LOW = -1e30
LANES = 128
MIB = 1024 * 1024
NT = (((1,), (1,)), ((), ()))


def pack_kernel(slots, q_ref, owner_ref, row_ref, out_ref, owner_held, row_held, sems):
    q_dev, cand = owner_ref.shape
    tokens = q_ref.shape[0]
    owners = out_ref.shape[0] - tokens
    copies = [
        pltpu.make_async_copy(source, target, sems.at[n])
        for n, (source, target) in enumerate(
            ((owner_ref, owner_held), (row_ref, row_held), (q_ref, out_ref.at[pl.ds(0, tokens)])))
    ]
    for copy in copies:
        copy.start()
    lane = lax.broadcasted_iota(jnp.int32, (q_dev, LANES), 1)
    own_q = lax.broadcasted_iota(jnp.int32, (q_dev, LANES), 0) == lane // cand
    spread = (
        lax.broadcasted_iota(jnp.int32, (cand, LANES), 0)
        == lax.broadcasted_iota(jnp.int32, (cand, LANES), 1) % cand
    ).astype(jnp.float32)
    earlier = (
        lax.broadcasted_iota(jnp.int32, (LANES, LANES), 0)
        < lax.broadcasted_iota(jnp.int32, (LANES, LANES), 1)
    ).astype(jnp.float32)
    number = lax.broadcasted_iota(jnp.int32, (1, LANES), 1).astype(jnp.float32) + 1.0
    each = lax.broadcasted_iota(jnp.int32, (owners, LANES), 0).astype(jnp.float32)
    place = lax.broadcasted_iota(jnp.int32, (LANES, LANES), 0).astype(jnp.float32)
    copies[0].wait()
    copies[1].wait()
    both = jnp.concatenate([owner_held[...], row_held[...]], axis=0).astype(jnp.float32)
    wide = jnp.dot(both, spread, preferred_element_type=jnp.float32)
    owner = jnp.sum(jnp.where(own_q, wide[:q_dev], 0.0), axis=0, keepdims=True)
    row = jnp.sum(jnp.where(own_q, wide[q_dev:], 0.0), axis=0, keepdims=True)
    hit = each == owner
    rank = jnp.dot(hit.astype(jnp.float32), earlier, preferred_element_type=jnp.float32)
    rank = jnp.sum(jnp.where(hit, rank, 0.0), axis=0, keepdims=True)
    rows = lax.dot_general(jnp.where(hit, row, 0.0), (place == rank).astype(jnp.float32), NT,
                           preferred_element_type=jnp.float32)
    numbers = lax.dot_general(jnp.where(hit, number, 0.0), (place == rank + slots).astype(jnp.float32), NT,
                              preferred_element_type=jnp.float32)
    out_ref[tokens:] = (rows + numbers).astype(out_ref.dtype)
    copies[2].wait()


def score_kernel(slots, qt, cand, jobs, outs, *refs):
    parts = len(jobs)
    all_refs, (cent_ref, held, len_ref) = refs[:parts], refs[parts:parts + 3]
    out_refs = refs[parts + 3:]
    out_refs = out_refs[len(out_refs) - outs:]
    height = all_refs[0].shape[1]
    tokens = out_refs[0].shape[2] - LANES
    owners = height - tokens
    ptok = held.shape[1]
    me = lax.axis_index("shard")
    mine = lax.broadcasted_iota(jnp.int32, (owners, LANES), 0) == me
    lens = jnp.broadcast_to(len_ref[...], (8, LANES))
    place = lax.broadcasted_iota(jnp.int32, (ptok, qt), 0)
    lane = lax.broadcasted_iota(jnp.int32, (1, LANES), 1) + 1

    def group(blocks):
        lines = []
        for ref, r, _, _ in blocks:
            table = ref[r, tokens:, :].astype(jnp.float32)
            lines.append(jnp.sum(jnp.where(mine, table, 0.0), axis=0, keepdims=True))
        lines.extend([jnp.zeros((1, LANES), jnp.float32)] * (8 - len(blocks)))
        lines = jnp.concatenate(lines, axis=0)
        row = lines.astype(jnp.int32)
        length = jnp.take_along_axis(lens, row, axis=1)
        number = pltpu.roll(lines, LANES - slots, 1)
        query = jnp.maximum(jnp.floor((number - 0.5) * (1.0 / cand)), 0.0).astype(jnp.int32)
        codes = row + (query << 8) + (number.astype(jnp.int32) << 16) + ((length - 1) << 24)
        for ref, r, out, at in blocks:
            scores = lax.dot_general(cent_ref[...], ref[r, :tokens, :], NT, preferred_element_type=jnp.float32)
            top = jnp.max(scores.reshape(-1, 8, tokens), axis=0)
            out[at, :, :tokens] = jnp.max(top, axis=0, keepdims=True)
        for n, (ref, r, out, at) in enumerate(blocks):
            total = jnp.full((1, LANES), LOW, jnp.float32)
            for slot in range(slots):
                code = codes[n, slot]
                first = pl.multiple_of(((code >> 8) & 255) * qt, qt)
                sim = lax.dot_general(held[code & 255], ref[r, pl.ds(first, qt), :], NT,
                                      preferred_element_type=jnp.float32)
                sim = jnp.where(place <= (code >> 24), sim, LOW)
                top = jnp.max(jnp.max(sim.reshape(-1, 8, qt), axis=0), axis=0, keepdims=True)
                score = jnp.sum(top, axis=1, keepdims=True) * (1.0 / qt)
                total = jnp.where(lane == ((code >> 16) & 255), score, total)
            out[at, :, tokens:] = total

    pieces = []
    for ref, job in zip(all_refs, jobs):
        count = ref.shape[0] // len(job)
        pieces.extend((ref, n * count, out_refs[which], at, count) for n, (which, at) in enumerate(job))
    blocks = [(ref, r + n, out, at + n) for ref, r, out, at, count in pieces for n in range(count)]
    if len(blocks) <= 8:
        group(blocks)
        return
    for ref, r, out, at, count in pieces:
        size = math.gcd(count, 8)

        def some(g, _, ref=ref, r=r, out=out, at=at, size=size):
            group([(ref, r + g * size + n, out, at + g * size + n) for n in range(size)])
            return _

        lax.fori_loop(0, count // size, some, 0)


def last_kernel(a_ref, b_ref, best_ref, sim_ref, best, sim, sems):
    q_dev, qt = best.shape
    cand = sim.shape[1]
    both = jnp.maximum(a_ref[0], b_ref[0])
    for q in range(q_dev):
        best[q:q + 1, :] = both[:, q * qt:(q + 1) * qt]
    copies = [pltpu.make_async_copy(best, best_ref, sems.at[0]), pltpu.make_async_copy(sim, sim_ref, sems.at[1])]
    copies[0].start()
    for q in range(q_dev):
        at = q_dev * qt + q * cand
        sim[q:q + 1, :] = both[:, at:at + cand]
    copies[1].start()
    for copy in copies:
        copy.wait()


def body(queries, centroids, passages, lengths, cand_owner, cand_row):
    q_dev, qt, dim = queries.shape
    cand = cand_row.shape[1]
    shards = lax.axis_size("shard")
    slots = 2 * q_dev * cand // shards
    tokens = q_dev * qt
    vmem = pl.BlockSpec(memory_space=pltpu.VMEM)
    hbm = pl.BlockSpec(memory_space=pltpu.HBM)
    owners = -(-shards // 16) * 16
    height = tokens + owners

    def stay(x):
        return pltpu.with_memory_space_constraint(x, pltpu.HBM)

    block = pl.pallas_call(
        functools.partial(pack_kernel, slots),
        out_shape=pltpu.VMEM((height, dim), queries.dtype),
        in_specs=[hbm] * 3,
        out_specs=vmem,
        scratch_shapes=[
            pltpu.VMEM((q_dev, cand), jnp.int32),
            pltpu.VMEM((q_dev, cand), jnp.int32),
            pltpu.SemaphoreType.DMA((3,)),
        ],
        compiler_params=pltpu.CompilerParams(vmem_limit_bytes=2 * MIB),
        cost_estimate=pl.CostEstimate(flops=int(1e10), bytes_accessed=1000, transcendentals=0),
        name="pack",
    )(stay(queries.reshape(tokens, dim)), stay(cand_owner.reshape(q_dev, cand)), stay(cand_row))

    index = tuple(pltpu.with_memory_space_constraint(x, pltpu.VMEM) for x in (centroids, passages, lengths))

    def swap(x, k):
        return lax.ppermute(x, "shard", [(i, i ^ k) for i in range(shards)])

    def score(blocks, jobs, *held):
        total = sum(b.shape[0] for b in blocks)
        wide = pltpu.VMEM((shards // 2, 1, tokens + q_dev * cand), jnp.float32)
        outs = len(held) or 2
        return pl.pallas_call(
            functools.partial(score_kernel, slots, qt, cand, jobs, outs),
            out_shape=[wide] * outs,
            in_specs=[vmem] * (len(blocks) + 3 + len(held)),
            out_specs=[vmem] * outs,
            input_output_aliases={len(blocks) + 3 + n: n for n in range(len(held))},
            compiler_params=pltpu.CompilerParams(vmem_limit_bytes=4 * MIB),
            cost_estimate=pl.CostEstimate(
                flops=4 * total * (tokens * centroids.size + slots * qt * (passages.size // passages.shape[0])),
                bytes_accessed=total * MIB, transcendentals=0),
            name="score",
        )(*blocks, *index, *held)

    far = []
    k = shards // 2
    while k > 2:
        far.append(k | 1)
        k //= 2
    first = block[None]
    for k in far[:-2]:
        first = jnp.concatenate([first, swap(first, k)], axis=0)
    f, g = far[-2:]
    d = g ^ 3 ^ 1
    piece = {0: first}
    for k in (f, 3, g, d):
        piece[k] = swap(first, k)
    for k in (d, 3, g):
        piece[f ^ k] = swap(piece[f], k)
    m = first.shape[0]

    def across(keys):
        return swap(jnp.concatenate([piece[k] for k in keys], axis=0), 1)

    column = (0, 1, f, f ^ 1, g, g ^ 1, f ^ g, f ^ g ^ 1)
    place = {k: (0, n * m) for n, k in enumerate(column)}
    place.update({k ^ 3: (1, n * m) for n, k in enumerate(column)})

    def jobs(*keys):
        return tuple(tuple(place[k] for k in (key if isinstance(key, tuple) else (key,))) for key in keys)

    def only(first, *keys):
        return tuple(tuple((0, at) for _, at in job) for job in jobs(first, *keys))

    xa, xb = (3, d), (f ^ 3, f ^ d)
    early = (0, f, g, 3, d)
    near, beyond = score([piece[k] for k in early], jobs(*early))
    beyond, piece[xb[0]], piece[xb[1]] = lax.optimization_barrier((beyond, piece[xb[0]], piece[xb[1]]))
    ca, cb = across(xa), across(xb)
    [beyond] = score([ca[:m], *(piece[k] for k in xb)], only(xa[0] ^ 1, *xb), beyond)
    beyond, cb, piece[f ^ g] = lax.optimization_barrier((beyond, cb, piece[f ^ g]))
    [beyond] = score([ca[m:], cb], only(xa[1] ^ 1, tuple(k ^ 1 for k in xb)), beyond)

    got = swap(beyond, 3)
    own = (0, f, g, f ^ g)
    cc = across(own)
    [near] = score([piece[f ^ g], cc], only(f ^ g, tuple(k ^ 1 for k in own)), near)
    near = jnp.maximum(near, got)
    for k in (g, f):
        half = near.shape[0] // 2
        near = jnp.maximum(near[:half], swap(near[half:], k))
    near = near.reshape(2, m, *near.shape[1:])
    for k in far[:-2][::-1]:
        half = near.shape[1] // 2
        near = jnp.maximum(near[:, :half], swap(near[:, half:], k))
    mine, got = near[0], swap(near[1], 1)
    return pl.pallas_call(
        last_kernel,
        out_shape=(jax.ShapeDtypeStruct((q_dev, qt), jnp.float32), jax.ShapeDtypeStruct((q_dev, cand), jnp.float32)),
        in_specs=[vmem] * 2,
        out_specs=(hbm, hbm),
        scratch_shapes=[
            pltpu.VMEM((q_dev, qt), jnp.float32),
            pltpu.VMEM((q_dev, cand), jnp.float32),
            pltpu.SemaphoreType.DMA((2,)),
        ],
        compiler_params=pltpu.CompilerParams(vmem_limit_bytes=MIB),
        name="last",
    )(mine, got)


def solution(mesh):
    both = ("groups", "shard")
    placed = (P(both, None, None), P(both, None), P(both, None, None), P(both, None), P(both, None, None), P(both, None))
    return jax.shard_map(body, mesh=mesh, in_specs=placed, out_specs=(P(both, None), P(both, None)), check_vma=False)
```

```python
import functools
import math

import jax
import jax.numpy as jnp
from jax import lax
from jax.experimental import pallas as pl
from jax.experimental.pallas import tpu as pltpu
from jax.sharding import PartitionSpec as P

LOW = -1e30
LANES = 128
MIB = 1024 * 1024
NT = (((1,), (1,)), ((), ()))


def pack_kernel(slots, q_ref, owner_ref, row_ref, out_ref, owner_held, row_held, sems):
    q_dev, cand = owner_ref.shape
    tokens = q_ref.shape[0]
    owners = out_ref.shape[0] - tokens
    copies = [
        pltpu.make_async_copy(source, target, sems.at[n])
        for n, (source, target) in enumerate(
            ((owner_ref, owner_held), (row_ref, row_held), (q_ref, out_ref.at[pl.ds(0, tokens)])))
    ]
    for copy in copies:
        copy.start()
    lane = lax.broadcasted_iota(jnp.int32, (q_dev, LANES), 1)
    own_q = lax.broadcasted_iota(jnp.int32, (q_dev, LANES), 0) == lane // cand
    spread = (
        lax.broadcasted_iota(jnp.int32, (cand, LANES), 0)
        == lax.broadcasted_iota(jnp.int32, (cand, LANES), 1) % cand
    ).astype(jnp.float32)
    earlier = (
        lax.broadcasted_iota(jnp.int32, (LANES, LANES), 0)
        < lax.broadcasted_iota(jnp.int32, (LANES, LANES), 1)
    ).astype(jnp.float32)
    number = lax.broadcasted_iota(jnp.int32, (1, LANES), 1).astype(jnp.float32) + 1.0
    each = lax.broadcasted_iota(jnp.int32, (owners, LANES), 0).astype(jnp.float32)
    place = lax.broadcasted_iota(jnp.int32, (LANES, LANES), 0).astype(jnp.float32)
    copies[0].wait()
    copies[1].wait()
    both = jnp.concatenate([owner_held[...], row_held[...]], axis=0).astype(jnp.float32)
    wide = jnp.dot(both, spread, preferred_element_type=jnp.float32)
    owner = jnp.sum(jnp.where(own_q, wide[:q_dev], 0.0), axis=0, keepdims=True)
    row = jnp.sum(jnp.where(own_q, wide[q_dev:], 0.0), axis=0, keepdims=True)
    hit = each == owner
    rank = jnp.dot(hit.astype(jnp.float32), earlier, preferred_element_type=jnp.float32)
    rank = jnp.sum(jnp.where(hit, rank, 0.0), axis=0, keepdims=True)
    rows = lax.dot_general(jnp.where(hit, row, 0.0), (place == rank).astype(jnp.float32), NT,
                           preferred_element_type=jnp.float32)
    numbers = lax.dot_general(jnp.where(hit, number, 0.0), (place == rank + slots).astype(jnp.float32), NT,
                              preferred_element_type=jnp.float32)
    out_ref[tokens:] = (rows + numbers).astype(out_ref.dtype)
    copies[2].wait()


def score_kernel(slots, qt, cand, jobs, outs, *refs):
    parts = len(jobs)
    all_refs, (cent_ref, held, len_ref) = refs[:parts], refs[parts:parts + 3]
    out_refs = refs[parts + 3:]
    out_refs = out_refs[len(out_refs) - outs:]
    height = all_refs[0].shape[1]
    tokens = out_refs[0].shape[2] - LANES
    owners = height - tokens
    ptok = held.shape[1]
    me = lax.axis_index("shard")
    mine = lax.broadcasted_iota(jnp.int32, (owners, LANES), 0) == me
    lens = jnp.broadcast_to(len_ref[...], (8, LANES))
    place = lax.broadcasted_iota(jnp.int32, (ptok, qt), 0)
    lane = lax.broadcasted_iota(jnp.int32, (1, LANES), 1) + 1

    def group(blocks):
        lines = []
        for ref, r, _, _ in blocks:
            table = ref[r, tokens:, :].astype(jnp.float32)
            lines.append(jnp.sum(jnp.where(mine, table, 0.0), axis=0, keepdims=True))
        lines.extend([jnp.zeros((1, LANES), jnp.float32)] * (8 - len(blocks)))
        lines = jnp.concatenate(lines, axis=0)
        row = lines.astype(jnp.int32)
        length = jnp.take_along_axis(lens, row, axis=1)
        number = pltpu.roll(lines, LANES - slots, 1)
        query = jnp.maximum(jnp.floor((number - 0.5) * (1.0 / cand)), 0.0).astype(jnp.int32)
        codes = row + (query << 8) + (number.astype(jnp.int32) << 16) + ((length - 1) << 24)
        for ref, r, out, at in blocks:
            scores = lax.dot_general(cent_ref[...], ref[r, :tokens, :], NT, preferred_element_type=jnp.float32)
            top = jnp.max(scores.reshape(-1, 8, tokens), axis=0)
            out[at, :, :tokens] = jnp.max(top, axis=0, keepdims=True)
        for n, (ref, r, out, at) in enumerate(blocks):
            total = jnp.full((1, LANES), LOW, jnp.float32)
            for slot in range(slots):
                code = codes[n, slot]
                first = pl.multiple_of(((code >> 8) & 255) * qt, qt)
                sim = lax.dot_general(held[code & 255], ref[r, pl.ds(first, qt), :], NT,
                                      preferred_element_type=jnp.float32)
                sim = jnp.where(place <= (code >> 24), sim, LOW)
                top = jnp.max(jnp.max(sim.reshape(-1, 8, qt), axis=0), axis=0, keepdims=True)
                score = jnp.sum(top, axis=1, keepdims=True) * (1.0 / qt)
                total = jnp.where(lane == ((code >> 16) & 255), score, total)
            out[at, :, tokens:] = total

    pieces = []
    for ref, job in zip(all_refs, jobs):
        count = ref.shape[0] // len(job)
        pieces.extend((ref, n * count, out_refs[which], at, count) for n, (which, at) in enumerate(job))
    blocks = [(ref, r + n, out, at + n) for ref, r, out, at, count in pieces for n in range(count)]
    if len(blocks) <= 8:
        group(blocks)
        return
    for ref, r, out, at, count in pieces:
        size = math.gcd(count, 8)

        def some(g, _, ref=ref, r=r, out=out, at=at, size=size):
            group([(ref, r + g * size + n, out, at + g * size + n) for n in range(size)])
            return _

        lax.fori_loop(0, count // size, some, 0)


def last_kernel(a_ref, b_ref, best_ref, sim_ref, best, sim, sems):
    q_dev, qt = best.shape
    cand = sim.shape[1]
    both = jnp.maximum(a_ref[0], b_ref[0])
    for q in range(q_dev):
        best[q:q + 1, :] = both[:, q * qt:(q + 1) * qt]
    copies = [pltpu.make_async_copy(best, best_ref, sems.at[0]), pltpu.make_async_copy(sim, sim_ref, sems.at[1])]
    copies[0].start()
    for q in range(q_dev):
        at = q_dev * qt + q * cand
        sim[q:q + 1, :] = both[:, at:at + cand]
    copies[1].start()
    for copy in copies:
        copy.wait()


def body(queries, centroids, passages, lengths, cand_owner, cand_row):
    q_dev, qt, dim = queries.shape
    cand = cand_row.shape[1]
    shards = lax.axis_size("shard")
    slots = 2 * q_dev * cand // shards
    tokens = q_dev * qt
    vmem = pl.BlockSpec(memory_space=pltpu.VMEM)
    hbm = pl.BlockSpec(memory_space=pltpu.HBM)
    owners = -(-shards // 16) * 16
    height = tokens + owners

    def stay(x):
        return pltpu.with_memory_space_constraint(x, pltpu.HBM)

    block = pl.pallas_call(
        functools.partial(pack_kernel, slots),
        out_shape=pltpu.VMEM((height, dim), queries.dtype),
        in_specs=[hbm] * 3,
        out_specs=vmem,
        scratch_shapes=[
            pltpu.VMEM((q_dev, cand), jnp.int32),
            pltpu.VMEM((q_dev, cand), jnp.int32),
            pltpu.SemaphoreType.DMA((3,)),
        ],
        compiler_params=pltpu.CompilerParams(vmem_limit_bytes=2 * MIB),
        cost_estimate=pl.CostEstimate(flops=int(1e10), bytes_accessed=1000, transcendentals=0),
        name="pack",
    )(stay(queries.reshape(tokens, dim)), stay(cand_owner.reshape(q_dev, cand)), stay(cand_row))

    index = tuple(pltpu.with_memory_space_constraint(x, pltpu.VMEM) for x in (centroids, passages, lengths))

    def swap(x, k):
        return lax.ppermute(x, "shard", [(i, i ^ k) for i in range(shards)])

    def score(blocks, jobs, *held):
        total = sum(b.shape[0] for b in blocks)
        wide = pltpu.VMEM((shards // 2, 1, tokens + q_dev * cand), jnp.float32)
        outs = len(held) or 2
        return pl.pallas_call(
            functools.partial(score_kernel, slots, qt, cand, jobs, outs),
            out_shape=[wide] * outs,
            in_specs=[vmem] * (len(blocks) + 3 + len(held)),
            out_specs=[vmem] * outs,
            input_output_aliases={len(blocks) + 3 + n: n for n in range(len(held))},
            compiler_params=pltpu.CompilerParams(vmem_limit_bytes=4 * MIB),
            cost_estimate=pl.CostEstimate(
                flops=4 * total * (tokens * centroids.size + slots * qt * (passages.size // passages.shape[0])),
                bytes_accessed=total * MIB, transcendentals=0),
            name="score",
        )(*blocks, *index, *held)

    far = []
    k = shards // 2
    while k > 2:
        far.append(k | 1)
        k //= 2
    first = block[None]
    for k in far[:-2]:
        first = jnp.concatenate([first, swap(first, k)], axis=0)
    f, g = far[-2:]
    d = g ^ 3 ^ 1
    piece = {0: first}
    for k in (f, 3, g, d):
        piece[k] = swap(first, k)
    for k in (d, 3, g):
        piece[f ^ k] = swap(piece[f], k)
    m = first.shape[0]

    def across(keys):
        return swap(jnp.concatenate([piece[k] for k in keys], axis=0), 1)

    column = (0, 1, f, f ^ 1, g, g ^ 1, f ^ g, f ^ g ^ 1)
    place = {k: (0, n * m) for n, k in enumerate(column)}
    place.update({k ^ 3: (1, n * m) for n, k in enumerate(column)})

    def jobs(*keys):
        return tuple(tuple(place[k] for k in (key if isinstance(key, tuple) else (key,))) for key in keys)

    def only(first, *keys):
        return tuple(tuple((0, at) for _, at in job) for job in jobs(first, *keys))

    xa, xb = (3, d), (f ^ 3, f ^ d)
    early = (0, f, g, 3, d)
    near, beyond = score([piece[k] for k in early], jobs(*early))
    beyond, piece[xb[0]], piece[xb[1]] = lax.optimization_barrier((beyond, piece[xb[0]], piece[xb[1]]))
    ca, cb = across(xa), across(xb)
    [beyond] = score([ca[:m], *(piece[k] for k in xb)], only(xa[0] ^ 1, *xb), beyond)
    beyond, cb = lax.optimization_barrier((beyond, cb))
    [beyond] = score([ca[m:], cb], only(xa[1] ^ 1, tuple(k ^ 1 for k in xb)), beyond)

    beyond, piece[f ^ g] = lax.optimization_barrier((beyond, piece[f ^ g]))
    got = swap(beyond, 3)
    own = (0, f, g, f ^ g)
    cc = across(own)
    alone = (f ^ g,)
    [near] = score([piece[k] for k in alone] + [cc], only(*alone, tuple(k ^ 1 for k in own)), near)
    near = jnp.maximum(near, got)
    for k in (g, f):
        half = near.shape[0] // 2
        near = jnp.maximum(near[:half], swap(near[half:], k))
    near = near.reshape(2, m, *near.shape[1:])
    for k in far[:-2][::-1]:
        half = near.shape[1] // 2
        near = jnp.maximum(near[:, :half], swap(near[:, half:], k))
    mine, got = near[0], swap(near[1], 1)
    return pl.pallas_call(
        last_kernel,
        out_shape=(jax.ShapeDtypeStruct((q_dev, qt), jnp.float32), jax.ShapeDtypeStruct((q_dev, cand), jnp.float32)),
        in_specs=[vmem] * 2,
        out_specs=(hbm, hbm),
        scratch_shapes=[
            pltpu.VMEM((q_dev, qt), jnp.float32),
            pltpu.VMEM((q_dev, cand), jnp.float32),
            pltpu.SemaphoreType.DMA((2,)),
        ],
        compiler_params=pltpu.CompilerParams(vmem_limit_bytes=MIB),
        name="last",
    )(mine, got)


def solution(mesh):
    both = ("groups", "shard")
    placed = (P(both, None, None), P(both, None), P(both, None, None), P(both, None), P(both, None, None), P(both, None))
    return jax.shard_map(body, mesh=mesh, in_specs=placed, out_specs=(P(both, None), P(both, None)), check_vma=False)
```

```python
import functools
import math

import jax
import jax.numpy as jnp
from jax import lax
from jax.experimental import pallas as pl
from jax.experimental.pallas import tpu as pltpu
from jax.sharding import PartitionSpec as P

LOW = -1e30
LANES = 128
MIB = 1024 * 1024
NT = (((1,), (1,)), ((), ()))


def pack_kernel(slots, q_ref, owner_ref, row_ref, out_ref, owner_held, row_held, sems):
    q_dev, cand = owner_ref.shape
    tokens = q_ref.shape[0]
    owners = out_ref.shape[0] - tokens
    copies = [
        pltpu.make_async_copy(source, target, sems.at[n])
        for n, (source, target) in enumerate(
            ((owner_ref, owner_held), (row_ref, row_held), (q_ref, out_ref.at[pl.ds(0, tokens)])))
    ]
    for copy in copies:
        copy.start()
    lane = lax.broadcasted_iota(jnp.int32, (q_dev, LANES), 1)
    own_q = lax.broadcasted_iota(jnp.int32, (q_dev, LANES), 0) == lane // cand
    spread = (
        lax.broadcasted_iota(jnp.int32, (cand, LANES), 0)
        == lax.broadcasted_iota(jnp.int32, (cand, LANES), 1) % cand
    ).astype(jnp.float32)
    earlier = (
        lax.broadcasted_iota(jnp.int32, (LANES, LANES), 0)
        < lax.broadcasted_iota(jnp.int32, (LANES, LANES), 1)
    ).astype(jnp.float32)
    number = lax.broadcasted_iota(jnp.int32, (1, LANES), 1).astype(jnp.float32) + 1.0
    each = lax.broadcasted_iota(jnp.int32, (owners, LANES), 0).astype(jnp.float32)
    place = lax.broadcasted_iota(jnp.int32, (LANES, LANES), 0).astype(jnp.float32)
    copies[0].wait()
    copies[1].wait()
    both = jnp.concatenate([owner_held[...], row_held[...]], axis=0).astype(jnp.float32)
    wide = jnp.dot(both, spread, preferred_element_type=jnp.float32)
    owner = jnp.sum(jnp.where(own_q, wide[:q_dev], 0.0), axis=0, keepdims=True)
    row = jnp.sum(jnp.where(own_q, wide[q_dev:], 0.0), axis=0, keepdims=True)
    hit = each == owner
    rank = jnp.dot(hit.astype(jnp.float32), earlier, preferred_element_type=jnp.float32)
    rank = jnp.sum(jnp.where(hit, rank, 0.0), axis=0, keepdims=True)
    rows = lax.dot_general(jnp.where(hit, row, 0.0), (place == rank).astype(jnp.float32), NT,
                           preferred_element_type=jnp.float32)
    numbers = lax.dot_general(jnp.where(hit, number, 0.0), (place == rank + slots).astype(jnp.float32), NT,
                              preferred_element_type=jnp.float32)
    out_ref[tokens:] = (rows + numbers).astype(out_ref.dtype)
    copies[2].wait()


def score_kernel(slots, qt, cand, jobs, outs, *refs):
    parts = len(jobs)
    all_refs, (cent_ref, held, len_ref) = refs[:parts], refs[parts:parts + 3]
    out_refs = refs[parts + 3:]
    out_refs = out_refs[len(out_refs) - outs:]
    height = all_refs[0].shape[1]
    tokens = out_refs[0].shape[2] - LANES
    owners = height - tokens
    ptok = held.shape[1]
    me = lax.axis_index("shard")
    mine = lax.broadcasted_iota(jnp.int32, (owners, LANES), 0) == me
    lens = jnp.broadcast_to(len_ref[...], (8, LANES))
    place = lax.broadcasted_iota(jnp.int32, (ptok, qt), 0)
    lane = lax.broadcasted_iota(jnp.int32, (1, LANES), 1) + 1

    def group(blocks):
        lines = []
        for ref, r, _, _ in blocks:
            table = ref[r, tokens:, :].astype(jnp.float32)
            lines.append(jnp.sum(jnp.where(mine, table, 0.0), axis=0, keepdims=True))
        lines.extend([jnp.zeros((1, LANES), jnp.float32)] * (8 - len(blocks)))
        lines = jnp.concatenate(lines, axis=0)
        row = lines.astype(jnp.int32)
        length = jnp.take_along_axis(lens, row, axis=1)
        number = pltpu.roll(lines, LANES - slots, 1)
        query = jnp.maximum(jnp.floor((number - 0.5) * (1.0 / cand)), 0.0).astype(jnp.int32)
        codes = row + (query << 8) + (number.astype(jnp.int32) << 16) + ((length - 1) << 24)
        for ref, r, out, at in blocks:
            scores = lax.dot_general(cent_ref[...], ref[r, :tokens, :], NT, preferred_element_type=jnp.float32)
            top = jnp.max(scores.reshape(-1, 8, tokens), axis=0)
            out[at, :, :tokens] = jnp.max(top, axis=0, keepdims=True)
        for n, (ref, r, out, at) in enumerate(blocks):
            total = jnp.full((1, LANES), LOW, jnp.float32)
            for slot in range(slots):
                code = codes[n, slot]
                first = pl.multiple_of(((code >> 8) & 255) * qt, qt)
                sim = lax.dot_general(held[code & 255], ref[r, pl.ds(first, qt), :], NT,
                                      preferred_element_type=jnp.float32)
                sim = jnp.where(place <= (code >> 24), sim, LOW)
                top = jnp.max(jnp.max(sim.reshape(-1, 8, qt), axis=0), axis=0, keepdims=True)
                score = jnp.sum(top, axis=1, keepdims=True) * (1.0 / qt)
                total = jnp.where(lane == ((code >> 16) & 255), score, total)
            out[at, :, tokens:] = total

    pieces = []
    for ref, job in zip(all_refs, jobs):
        count = ref.shape[0] // len(job)
        pieces.extend((ref, n * count, out_refs[which], at, count) for n, (which, at) in enumerate(job))
    blocks = [(ref, r + n, out, at + n) for ref, r, out, at, count in pieces for n in range(count)]
    if len(blocks) <= 8:
        group(blocks)
        return
    for ref, r, out, at, count in pieces:
        size = math.gcd(count, 8)

        def some(g, _, ref=ref, r=r, out=out, at=at, size=size):
            group([(ref, r + g * size + n, out, at + g * size + n) for n in range(size)])
            return _

        lax.fori_loop(0, count // size, some, 0)


def last_kernel(a_ref, b_ref, best_ref, sim_ref, best, sim, sems):
    q_dev, qt = best.shape
    cand = sim.shape[1]
    both = jnp.maximum(a_ref[0], b_ref[0])
    for q in range(q_dev):
        best[q:q + 1, :] = both[:, q * qt:(q + 1) * qt]
    copies = [pltpu.make_async_copy(best, best_ref, sems.at[0]), pltpu.make_async_copy(sim, sim_ref, sems.at[1])]
    copies[0].start()
    for q in range(q_dev):
        at = q_dev * qt + q * cand
        sim[q:q + 1, :] = both[:, at:at + cand]
    copies[1].start()
    for copy in copies:
        copy.wait()


def body(queries, centroids, passages, lengths, cand_owner, cand_row):
    q_dev, qt, dim = queries.shape
    cand = cand_row.shape[1]
    shards = lax.axis_size("shard")
    slots = 2 * q_dev * cand // shards
    tokens = q_dev * qt
    vmem = pl.BlockSpec(memory_space=pltpu.VMEM)
    hbm = pl.BlockSpec(memory_space=pltpu.HBM)
    owners = -(-shards // 16) * 16
    height = tokens + owners

    def stay(x):
        return pltpu.with_memory_space_constraint(x, pltpu.HBM)

    block = pl.pallas_call(
        functools.partial(pack_kernel, slots),
        out_shape=pltpu.VMEM((height, dim), queries.dtype),
        in_specs=[hbm] * 3,
        out_specs=vmem,
        scratch_shapes=[
            pltpu.VMEM((q_dev, cand), jnp.int32),
            pltpu.VMEM((q_dev, cand), jnp.int32),
            pltpu.SemaphoreType.DMA((3,)),
        ],
        compiler_params=pltpu.CompilerParams(vmem_limit_bytes=2 * MIB),
        cost_estimate=pl.CostEstimate(flops=int(1e10), bytes_accessed=1000, transcendentals=0),
        name="pack",
    )(stay(queries.reshape(tokens, dim)), stay(cand_owner.reshape(q_dev, cand)), stay(cand_row))

    index = tuple(pltpu.with_memory_space_constraint(x, pltpu.VMEM) for x in (centroids, passages, lengths))

    def swap(x, k):
        return lax.ppermute(x, "shard", [(i, i ^ k) for i in range(shards)])

    def score(blocks, jobs, *held):
        total = sum(b.shape[0] for b in blocks)
        wide = pltpu.VMEM((shards // 2, 1, tokens + q_dev * cand), jnp.float32)
        outs = len(held) or 2
        return pl.pallas_call(
            functools.partial(score_kernel, slots, qt, cand, jobs, outs),
            out_shape=[wide] * outs,
            in_specs=[vmem] * (len(blocks) + 3 + len(held)),
            out_specs=[vmem] * outs,
            input_output_aliases={len(blocks) + 3 + n: n for n in range(len(held))},
            compiler_params=pltpu.CompilerParams(vmem_limit_bytes=4 * MIB),
            cost_estimate=pl.CostEstimate(
                flops=4 * total * (tokens * centroids.size + slots * qt * (passages.size // passages.shape[0])),
                bytes_accessed=total * MIB, transcendentals=0),
            name="score",
        )(*blocks, *index, *held)

    far = []
    k = shards // 2
    while k > 2:
        far.append(k | 1)
        k //= 2
    first = block[None]
    for k in far[:-2]:
        first = jnp.concatenate([first, swap(first, k)], axis=0)
    f, g = far[-2:]
    d = g ^ 3 ^ 1
    piece = {0: first}
    for k in (f, 3, g, d):
        piece[k] = swap(first, k)
    for k in (d, 3, g):
        piece[f ^ k] = swap(piece[f], k)
    m = first.shape[0]

    def across(keys):
        return swap(jnp.concatenate([piece[k] for k in keys], axis=0), 1)

    column = (0, 1, f, f ^ 1, g, g ^ 1, f ^ g, f ^ g ^ 1)
    place = {k: (0, n * m) for n, k in enumerate(column)}
    place.update({k ^ 3: (1, n * m) for n, k in enumerate(column)})

    def jobs(*keys):
        return tuple(tuple(place[k] for k in (key if isinstance(key, tuple) else (key,))) for key in keys)

    def only(first, *keys):
        return tuple(tuple((0, at) for _, at in job) for job in jobs(first, *keys))

    xa, xb = (3, d), (f ^ 3, f ^ d)
    early = (f, g, 3, d)
    near, beyond = score([piece[k] for k in early], jobs(*early))
    beyond, piece[xb[0]], piece[xb[1]] = lax.optimization_barrier((beyond, piece[xb[0]], piece[xb[1]]))
    ca, cb = across(xa), across(xb)
    [beyond] = score([ca[:m], *(piece[k] for k in xb)], only(xa[0] ^ 1, *xb), beyond)
    beyond, cb = lax.optimization_barrier((beyond, cb))
    [beyond] = score([ca[m:], cb], only(xa[1] ^ 1, tuple(k ^ 1 for k in xb)), beyond)

    beyond, piece[f ^ g] = lax.optimization_barrier((beyond, piece[f ^ g]))
    got = swap(beyond, 3)
    own = (0, f, g, f ^ g)
    cc = across(own)
    alone = (0, f ^ g,)
    [near] = score([piece[k] for k in alone], only(*alone), near)
    near, cc = lax.optimization_barrier((near, cc))
    [near] = score([cc], only(tuple(k ^ 1 for k in own)), near)
    near = jnp.maximum(near, got)
    for k in (g, f):
        half = near.shape[0] // 2
        near = jnp.maximum(near[:half], swap(near[half:], k))
    near = near.reshape(2, m, *near.shape[1:])
    for k in far[:-2][::-1]:
        half = near.shape[1] // 2
        near = jnp.maximum(near[:, :half], swap(near[:, half:], k))
    mine, got = near[0], swap(near[1], 1)
    return pl.pallas_call(
        last_kernel,
        out_shape=(jax.ShapeDtypeStruct((q_dev, qt), jnp.float32), jax.ShapeDtypeStruct((q_dev, cand), jnp.float32)),
        in_specs=[vmem] * 2,
        out_specs=(hbm, hbm),
        scratch_shapes=[
            pltpu.VMEM((q_dev, qt), jnp.float32),
            pltpu.VMEM((q_dev, cand), jnp.float32),
            pltpu.SemaphoreType.DMA((2,)),
        ],
        compiler_params=pltpu.CompilerParams(vmem_limit_bytes=MIB),
        name="last",
    )(mine, got)


def solution(mesh):
    both = ("groups", "shard")
    placed = (P(both, None, None), P(both, None), P(both, None, None), P(both, None), P(both, None, None), P(both, None))
    return jax.shard_map(body, mesh=mesh, in_specs=placed, out_specs=(P(both, None), P(both, None)), check_vma=False)
```

```python
import functools
import math

import jax
import jax.numpy as jnp
from jax import lax
from jax.experimental import pallas as pl
from jax.experimental.pallas import tpu as pltpu
from jax.sharding import PartitionSpec as P

LOW = -1e30
LANES = 128
MIB = 1024 * 1024
NT = (((1,), (1,)), ((), ()))


def pack_kernel(slots, q_ref, owner_ref, row_ref, out_ref, owner_held, row_held, sems):
    q_dev, cand = owner_ref.shape
    tokens = q_ref.shape[0]
    owners = out_ref.shape[0] - tokens
    copies = [
        pltpu.make_async_copy(source, target, sems.at[n])
        for n, (source, target) in enumerate(
            ((owner_ref, owner_held), (row_ref, row_held), (q_ref, out_ref.at[pl.ds(0, tokens)])))
    ]
    for copy in copies:
        copy.start()
    lane = lax.broadcasted_iota(jnp.int32, (q_dev, LANES), 1)
    own_q = lax.broadcasted_iota(jnp.int32, (q_dev, LANES), 0) == lane // cand
    spread = (
        lax.broadcasted_iota(jnp.int32, (cand, LANES), 0)
        == lax.broadcasted_iota(jnp.int32, (cand, LANES), 1) % cand
    ).astype(jnp.float32)
    earlier = (
        lax.broadcasted_iota(jnp.int32, (LANES, LANES), 0)
        < lax.broadcasted_iota(jnp.int32, (LANES, LANES), 1)
    ).astype(jnp.float32)
    number = lax.broadcasted_iota(jnp.int32, (1, LANES), 1).astype(jnp.float32) + 1.0
    each = lax.broadcasted_iota(jnp.int32, (owners, LANES), 0).astype(jnp.float32)
    place = lax.broadcasted_iota(jnp.int32, (LANES, LANES), 0).astype(jnp.float32)
    copies[0].wait()
    copies[1].wait()
    both = jnp.concatenate([owner_held[...], row_held[...]], axis=0).astype(jnp.float32).astype(jnp.bfloat16)
    wide = jnp.dot(both, spread.astype(jnp.bfloat16), preferred_element_type=jnp.float32)
    owner = jnp.sum(jnp.where(own_q, wide[:q_dev], 0.0), axis=0, keepdims=True)
    row = jnp.sum(jnp.where(own_q, wide[q_dev:], 0.0), axis=0, keepdims=True)
    hit = each == owner
    rank = jnp.dot(hit.astype(jnp.bfloat16), earlier.astype(jnp.bfloat16), preferred_element_type=jnp.float32)
    rank = jnp.sum(jnp.where(hit, rank, 0.0), axis=0, keepdims=True)
    rows = lax.dot_general(jnp.where(hit, row, 0.0).astype(jnp.bfloat16), (place == rank).astype(jnp.bfloat16), NT,
                           preferred_element_type=jnp.float32)
    numbers = lax.dot_general(jnp.where(hit, number, 0.0).astype(jnp.bfloat16), (place == rank + slots).astype(jnp.bfloat16), NT,
                              preferred_element_type=jnp.float32)
    out_ref[tokens:] = (rows + numbers).astype(out_ref.dtype)
    copies[2].wait()


def score_kernel(slots, qt, cand, jobs, outs, *refs):
    parts = len(jobs)
    all_refs, (cent_ref, held, len_ref) = refs[:parts], refs[parts:parts + 3]
    out_refs = refs[parts + 3:]
    out_refs = out_refs[len(out_refs) - outs:]
    height = all_refs[0].shape[1]
    tokens = out_refs[0].shape[2] - LANES
    owners = height - tokens
    ptok = held.shape[1]
    me = lax.axis_index("shard")
    mine = lax.broadcasted_iota(jnp.int32, (owners, LANES), 0) == me
    lens = jnp.broadcast_to(len_ref[...], (8, LANES))
    place = lax.broadcasted_iota(jnp.int32, (ptok, qt), 0)
    lane = lax.broadcasted_iota(jnp.int32, (1, LANES), 1) + 1

    def group(blocks):
        lines = []
        for ref, r, _, _ in blocks:
            table = ref[r, tokens:, :].astype(jnp.float32)
            lines.append(jnp.sum(jnp.where(mine, table, 0.0), axis=0, keepdims=True))
        lines.extend([jnp.zeros((1, LANES), jnp.float32)] * (8 - len(blocks)))
        lines = jnp.concatenate(lines, axis=0)
        row = lines.astype(jnp.int32)
        length = jnp.take_along_axis(lens, row, axis=1)
        number = pltpu.roll(lines, LANES - slots, 1)
        query = jnp.maximum(jnp.floor((number - 0.5) * (1.0 / cand)), 0.0).astype(jnp.int32)
        codes = row + (query << 8) + (number.astype(jnp.int32) << 16) + ((length - 1) << 24)
        for ref, r, out, at in blocks:
            scores = lax.dot_general(cent_ref[...], ref[r, :tokens, :], NT, preferred_element_type=jnp.float32)
            top = jnp.max(scores.reshape(-1, 8, tokens), axis=0)
            out[at, :, :tokens] = jnp.max(top, axis=0, keepdims=True)
        for n, (ref, r, out, at) in enumerate(blocks):
            total = jnp.full((1, LANES), LOW, jnp.float32)
            for slot in range(slots):
                code = codes[n, slot]
                first = pl.multiple_of(((code >> 8) & 255) * qt, qt)
                sim = lax.dot_general(held[code & 255], ref[r, pl.ds(first, qt), :], NT,
                                      preferred_element_type=jnp.float32)
                sim = jnp.where(place <= (code >> 24), sim, LOW)
                top = jnp.max(jnp.max(sim.reshape(-1, 8, qt), axis=0), axis=0, keepdims=True)
                score = jnp.sum(top, axis=1, keepdims=True) * (1.0 / qt)
                total = jnp.where(lane == ((code >> 16) & 255), score, total)
            out[at, :, tokens:] = total

    pieces = []
    for ref, job in zip(all_refs, jobs):
        count = ref.shape[0] // len(job)
        pieces.extend((ref, n * count, out_refs[which], at, count) for n, (which, at) in enumerate(job))
    blocks = [(ref, r + n, out, at + n) for ref, r, out, at, count in pieces for n in range(count)]
    if len(blocks) <= 8:
        group(blocks)
        return
    for ref, r, out, at, count in pieces:
        size = math.gcd(count, 8)

        def some(g, _, ref=ref, r=r, out=out, at=at, size=size):
            group([(ref, r + g * size + n, out, at + g * size + n) for n in range(size)])
            return _

        lax.fori_loop(0, count // size, some, 0)


def last_kernel(a_ref, b_ref, best_ref, sim_ref, best, sim, sems):
    q_dev, qt = best.shape
    cand = sim.shape[1]
    both = jnp.maximum(a_ref[0], b_ref[0])
    for q in range(q_dev):
        best[q:q + 1, :] = both[:, q * qt:(q + 1) * qt]
    copies = [pltpu.make_async_copy(best, best_ref, sems.at[0]), pltpu.make_async_copy(sim, sim_ref, sems.at[1])]
    copies[0].start()
    for q in range(q_dev):
        at = q_dev * qt + q * cand
        sim[q:q + 1, :] = both[:, at:at + cand]
    copies[1].start()
    for copy in copies:
        copy.wait()


def body(queries, centroids, passages, lengths, cand_owner, cand_row):
    q_dev, qt, dim = queries.shape
    cand = cand_row.shape[1]
    shards = lax.axis_size("shard")
    slots = 2 * q_dev * cand // shards
    tokens = q_dev * qt
    vmem = pl.BlockSpec(memory_space=pltpu.VMEM)
    hbm = pl.BlockSpec(memory_space=pltpu.HBM)
    owners = -(-shards // 16) * 16
    height = tokens + owners

    def stay(x):
        return pltpu.with_memory_space_constraint(x, pltpu.HBM)

    block = pl.pallas_call(
        functools.partial(pack_kernel, slots),
        out_shape=pltpu.VMEM((height, dim), queries.dtype),
        in_specs=[hbm] * 3,
        out_specs=vmem,
        scratch_shapes=[
            pltpu.VMEM((q_dev, cand), jnp.int32),
            pltpu.VMEM((q_dev, cand), jnp.int32),
            pltpu.SemaphoreType.DMA((3,)),
        ],
        compiler_params=pltpu.CompilerParams(vmem_limit_bytes=2 * MIB),
        cost_estimate=pl.CostEstimate(flops=int(1e10), bytes_accessed=1000, transcendentals=0),
        name="pack",
    )(stay(queries.reshape(tokens, dim)), stay(cand_owner.reshape(q_dev, cand)), stay(cand_row))

    index = tuple(pltpu.with_memory_space_constraint(x, pltpu.VMEM) for x in (centroids, passages, lengths))

    def swap(x, k):
        return lax.ppermute(x, "shard", [(i, i ^ k) for i in range(shards)])

    def score(blocks, jobs, *held):
        total = sum(b.shape[0] for b in blocks)
        wide = pltpu.VMEM((shards // 2, 1, tokens + q_dev * cand), jnp.float32)
        outs = len(held) or 2
        return pl.pallas_call(
            functools.partial(score_kernel, slots, qt, cand, jobs, outs),
            out_shape=[wide] * outs,
            in_specs=[vmem] * (len(blocks) + 3 + len(held)),
            out_specs=[vmem] * outs,
            input_output_aliases={len(blocks) + 3 + n: n for n in range(len(held))},
            compiler_params=pltpu.CompilerParams(vmem_limit_bytes=4 * MIB),
            cost_estimate=pl.CostEstimate(
                flops=4 * total * (tokens * centroids.size + slots * qt * (passages.size // passages.shape[0])),
                bytes_accessed=total * MIB, transcendentals=0),
            name="score",
        )(*blocks, *index, *held)

    far = []
    k = shards // 2
    while k > 2:
        far.append(k | 1)
        k //= 2
    first = block[None]
    for k in far[:-2]:
        first = jnp.concatenate([first, swap(first, k)], axis=0)
    f, g = far[-2:]
    d = g ^ 3 ^ 1
    piece = {0: first}
    for k in (f, 3, g, d):
        piece[k] = swap(first, k)
    for k in (d, 3, g):
        piece[f ^ k] = swap(piece[f], k)
    m = first.shape[0]

    def across(keys):
        return swap(jnp.concatenate([piece[k] for k in keys], axis=0), 1)

    column = (0, 1, g, g ^ 1, f, f ^ 1, f ^ g, f ^ g ^ 1)
    place = {k: (0, n * m) for n, k in enumerate(column)}
    place.update({k ^ 3: (1, n * m) for n, k in enumerate(column)})

    def jobs(*keys):
        return tuple(tuple(place[k] for k in (key if isinstance(key, tuple) else (key,))) for key in keys)

    def only(first, *keys):
        return tuple(tuple((0, at) for _, at in job) for job in jobs(first, *keys))

    xa, xb = (3, d), (f ^ 3, f ^ d)
    early = (0, f, g, 3, d)
    near, beyond = score([piece[k] for k in early], jobs(*early))
    beyond, piece[xb[0]], piece[xb[1]] = lax.optimization_barrier((beyond, piece[xb[0]], piece[xb[1]]))
    ca, cb = across(xa), across(xb)
    [beyond] = score([ca[:m], *(piece[k] for k in xb)], only(xa[0] ^ 1, *xb), beyond)
    beyond, cb = lax.optimization_barrier((beyond, cb))
    [beyond] = score([ca[m:], cb], only(xa[1] ^ 1, tuple(k ^ 1 for k in xb)), beyond)

    beyond, piece[f ^ g] = lax.optimization_barrier((beyond, piece[f ^ g]))
    got = swap(beyond, 3)
    own = (0, f, g, f ^ g)
    cc = across(own)
    alone = (f ^ g,)
    [near] = score([piece[k] for k in alone] + [cc], only(*alone, tuple(k ^ 1 for k in own)), near)
    near = jnp.maximum(near, got)
    for k in (f, g):
        half = near.shape[0] // 2
        near = jnp.maximum(near[:half], swap(near[half:], k))
    near = near.reshape(2, m, *near.shape[1:])
    for k in far[:-2][::-1]:
        half = near.shape[1] // 2
        near = jnp.maximum(near[:, :half], swap(near[:, half:], k))
    mine, got = near[0], swap(near[1], 1)
    return pl.pallas_call(
        last_kernel,
        out_shape=(jax.ShapeDtypeStruct((q_dev, qt), jnp.float32), jax.ShapeDtypeStruct((q_dev, cand), jnp.float32)),
        in_specs=[vmem] * 2,
        out_specs=(hbm, hbm),
        scratch_shapes=[
            pltpu.VMEM((q_dev, qt), jnp.float32),
            pltpu.VMEM((q_dev, cand), jnp.float32),
            pltpu.SemaphoreType.DMA((2,)),
        ],
        compiler_params=pltpu.CompilerParams(vmem_limit_bytes=MIB),
        name="last",
    )(mine, got)


def solution(mesh):
    both = ("groups", "shard")
    placed = (P(both, None, None), P(both, None), P(both, None, None), P(both, None), P(both, None, None), P(both, None))
    return jax.shard_map(body, mesh=mesh, in_specs=placed, out_specs=(P(both, None), P(both, None)), check_vma=False)
```
